128 devices in a mesh: seq: 8 (over x, y_lo), dp: 16 (over y_hi, z, core).
Axes of the slice: x: 4, y: 4 (y_hi: 2, y_lo: 2; y = y_hi * 2 + y_lo), z: 4, core: 2. Of those that a mesh axis runs over, the one named last changes fastest.
Arguments:
- tokens: bfloat16 [16, 8192, 1024], P('dp', 'seq'), may hold values from -6 to 6
- w_qkv: bfloat16 [1024, 3072], replicated
- offsets: int32 [16, 16], P('dp'), may hold values from 0 to 7, as said below
- d_attended: bfloat16 [16, 8192, 1024], P('dp', 'seq'), may hold values from -6 to 6
Outputs:
- attended: bfloat16 [16, 8192, 1024], P('dp', 'seq')
- d_tokens: bfloat16 [16, 8192, 1024], P('dp', 'seq')
- d_weights: float32 [1024, 3072], P('seq')
The draws below stay inside these ranges and needn't reach their ends.
Inputs may be any that keep to these rules, and one draw needn't show every extreme that they name: offsets[n, h] is below min(2 ** (h // 4), 8), the span of head h's group.
All inputs are finite; a program needn't handle non-finite values.
Results may differ from the reference program's by a relative error of at most 0.039.
The reference program's roundings to bfloat16 on the way count: a program that leaves them out, or rounds other values in their place, can miss the bound.
Values may be sent and summed in bfloat16 or wider, within the bound.
No kernel may reach another device: no remote copies, remote signals or barrier semaphores. Data moves between devices by JAX's collectives and lax.ppermute only.
A program may use at most 128 MiB of HBM per device.

```python
import jax
import jax.numpy as jnp
from jax import lax

D = 1024
HEADS = 16
HEAD_DIM = 64
BLK = 128
TOK_DEV = 1024
LEN = 8192
SEQS = 16
N_SEQ = 8


def draw_w_qkv(key, part):
    key = jax.random.fold_in(key, 11)
    first_key, second_key, third_key = jax.random.split(key, 3)
    factor = D ** (-0.5)
    queries = jax.random.normal(first_key, (D, D), jnp.float32) * factor
    keys_part = jax.random.normal(second_key, (D, D), jnp.float32) * factor
    values = jax.random.normal(third_key, (D, D), jnp.float32) * factor
    return jnp.concatenate([queries, keys_part, values], axis=1).astype(jnp.bfloat16)


def draw_offsets(key, part):
    key = jax.random.fold_in(key, 23)
    spans = jnp.minimum(2 ** (jnp.arange(HEADS) // (HEADS // 4)), N_SEQ)
    drawn = jax.random.randint(key, (SEQS, HEADS), 0, 1 << 20)
    picked = drawn % spans[None, :]
    return picked.at[0, HEADS - 1].set(spans[HEADS - 1] - 1).astype(jnp.int32)


def with_spikes(values, rng, source, target, parts, factor):
    def block_of(position):
        return (jnp.arange(values.shape[position]) // (values.shape[position] // parts)).reshape((-1,) + (1,) * (values.ndim - 1 - position))

    one_side = jax.random.permutation(rng, parts)[block_of(target)]
    second = (block_of(target) + parts // 2) % parts
    return jnp.where((block_of(source) == one_side) | (block_of(source) == second), factor * values, values)


def block_levels(stream_key, shape, pieces, smallest, largest):
    factor_of = 1.0
    for dim, blocks in pieces:
        steps = jax.random.uniform(jax.random.fold_in(jax.random.fold_in(stream_key, 6), dim), (blocks,), jnp.float32, smallest / len(pieces), largest / len(pieces))
        factor_of = factor_of * jnp.repeat(jnp.exp(steps), shape[dim] // blocks).reshape((-1,) + (1,) * (len(shape) - 1 - dim))
    return factor_of


def centred(rng, extent, scale, reach, pieces=(), kind=jnp.bfloat16):
    values = scale * jax.random.normal(rng, extent, jnp.float32)
    if pieces:
        values = values * block_levels(rng, extent, pieces, -0.22, 0.18)
    return jnp.clip(values, -reach, reach).astype(kind)


def bell_draw_with(key, shape, width, limit, cuts, heavy, kind=jnp.bfloat16):
    entries = width * jax.random.normal(key, shape, jnp.float32)
    if cuts:
        entries = entries * block_levels(key, shape, cuts, -0.22, 0.18)
    return jnp.clip(with_spikes(entries, jax.random.fold_in(key, 3), *heavy), -limit, limit).astype(kind)


def setup_inputs(seed: int = 0) -> dict:
    splits = jax.random.split(jax.random.key(seed), 5)
    return {
        "tokens": bell_draw_with(splits[0], (SEQS, LEN, D), 1.0, 6.0, ((0, 16), (1, 8)), (1, 2, 8, 2.0)),
        "w_qkv": draw_w_qkv(jax.random.fold_in(splits[4], 71), 0),
        "offsets": draw_offsets(jax.random.fold_in(splits[4], 71), 0),
        "d_attended": centred(splits[3], (SEQS, LEN, D), 1.0, 6.0, ((0, 16), (1, 8))),
    }


def product(form, left, right):
    return jnp.einsum(form, left.astype(jnp.float32), right.astype(jnp.float32))


def select(row_block, chosen):
    span = chosen.shape[0]
    row_total, columns = row_block.shape
    blocks = row_block.reshape(row_total // (BLK * span), span, BLK, columns)
    picked = jnp.sum(jnp.where(chosen[None, :, None, :], blocks, jnp.zeros((), row_block.dtype)), axis=1)
    return picked.astype(row_block.dtype).reshape(row_total // span, columns)


def spread(compact, chosen):
    columns = compact.shape[1]
    blocks = compact.reshape(-1, 1, BLK, columns)
    full = jnp.where(chosen[None, :, None, :], blocks, jnp.zeros((), compact.dtype))
    return full.reshape(-1, columns)


def scores_of(query, keys, positions):
    row_total, columns = query.shape
    heads_here = columns // HEAD_DIM
    query3 = query.reshape(row_total, heads_here, HEAD_DIM)
    keys3 = keys.reshape(keys.shape[0], heads_here, HEAD_DIM)
    return product("qhd,khd->hqk", query3, keys3) * 0.125


def attend(query, keys, values, positions):
    row_total, columns = query.shape
    heads_here = columns // HEAD_DIM
    scores = scores_of(query, keys, positions)
    highest = jnp.max(scores, axis=2, keepdims=True)
    row_sums = jnp.sum(jnp.exp(scores - highest), axis=2, keepdims=True)
    log_total = highest + jnp.log(row_sums)
    attention_b = jnp.exp(scores - log_total).astype(jnp.bfloat16)
    values3 = values.reshape(values.shape[0], heads_here, HEAD_DIM)
    output = product("hqk,khd->qhd", attention_b, values3)
    return output.reshape(row_total, columns).astype(jnp.bfloat16), log_total


def attend_back(query, keys, values, positions, log_total, output, incoming):
    row_total, columns = query.shape
    heads_here = columns // HEAD_DIM
    scores = scores_of(query, keys, positions)
    attention = jnp.exp(scores - log_total)
    attention_b = attention.astype(jnp.bfloat16)
    query3 = query.reshape(row_total, heads_here, HEAD_DIM)
    keys3 = keys.reshape(keys.shape[0], heads_here, HEAD_DIM)
    values3 = values.reshape(values.shape[0], heads_here, HEAD_DIM)
    incoming3 = incoming.reshape(row_total, heads_here, HEAD_DIM)
    output3 = output.reshape(row_total, heads_here, HEAD_DIM)
    grad_prob = product("qhd,khd->hqk", incoming3, values3)
    delta = jnp.sum(incoming3.astype(jnp.float32) * output3.astype(jnp.float32), axis=2)
    grad_score = (attention * (grad_prob - jnp.transpose(delta)[:, :, None])).astype(jnp.bfloat16)
    grad_query = product("hqk,khd->qhd", grad_score, keys3) * 0.125
    grad_keys = product("hqk,qhd->khd", grad_score, query3) * 0.125
    grad_values = product("hqk,qhd->khd", attention_b, incoming3)
    return (grad_query.reshape(row_total, columns), grad_keys.reshape(-1, columns), grad_values.reshape(-1, columns))


def one_sequence(inputs, incoming, offset_row, w_qkv):
    qkv = jnp.dot(inputs, w_qkv, preferred_element_type=jnp.float32).astype(jnp.bfloat16)
    per_group = HEADS // 4
    columns = per_group * HEAD_DIM
    outputs, grad_q, grad_k, grad_v = [], [], [], []
    for group in range(4):
        span = min(2 ** group, N_SEQ)
        first_col = group * columns
        column_offsets = jnp.repeat(offset_row[group * per_group:(group + 1) * per_group], HEAD_DIM)
        chosen = jnp.arange(span)[:, None] == column_offsets[None, :]
        segments = LEN // (span * TOK_DEV)
        query = select(qkv[:, first_col:first_col + columns], chosen).reshape(segments, TOK_DEV, columns)
        keys = select(qkv[:, D + first_col:D + first_col + columns], chosen).reshape(segments, TOK_DEV, columns)
        values = select(qkv[:, 2 * D + first_col:2 * D + first_col + columns], chosen).reshape(segments, TOK_DEV, columns)
        grads_in = select(incoming[:, first_col:first_col + columns], chosen).reshape(segments, TOK_DEV, columns)
        positions = jnp.arange(TOK_DEV)

        def segment_step(items):
            seg_q, seg_k, seg_v, seg_g = items
            result, log_total = attend(seg_q, seg_k, seg_v, positions)
            back_q, back_k, back_v = attend_back(seg_q, seg_k, seg_v, positions, log_total, result, seg_g)
            return result, back_q, back_k, back_v

        result, back_q, back_k, back_v = lax.map(segment_step, (query, keys, values, grads_in))
        outputs.append(spread(result.reshape(-1, columns), chosen))
        grad_q.append(spread(back_q.reshape(-1, columns), chosen))
        grad_k.append(spread(back_k.reshape(-1, columns), chosen))
        grad_v.append(spread(back_v.reshape(-1, columns), chosen))
    attended = jnp.concatenate(outputs, axis=1)
    d_qkv = jnp.concatenate(grad_q + grad_k + grad_v, axis=1).astype(jnp.bfloat16)
    d_inputs = jnp.dot(d_qkv, w_qkv.T, preferred_element_type=jnp.float32).astype(jnp.bfloat16)
    d_weight_part = jnp.dot(inputs.T, d_qkv, preferred_element_type=jnp.float32)
    return attended, d_inputs, d_weight_part


def reference(tokens, w_qkv, offsets, d_attended):
    def seq_step(carry, items):
        inputs, incoming, offset_row = items
        attended, d_inputs, d_weight_part = one_sequence(inputs, incoming, offset_row, w_qkv)
        return carry + d_weight_part, (attended, d_inputs)

    start_carry = jnp.zeros((D, 3 * D), jnp.float32)
    summed, (attended, d_tokens) = lax.scan(seq_step, start_carry, (tokens, d_attended, offsets))
    return attended, d_tokens, summed
```

```python
import jax
import jax.numpy as jnp
from jax import lax
from jax.experimental import pallas as pl
from jax.experimental.pallas import tpu as pltpu
from jax.sharding import PartitionSpec as P

BLK = 128
ROWS = 1024
BF = jnp.bfloat16
F32 = jnp.float32
SPANS = (1, 2, 4, 8)
CHUNK = 256
VMEM_LIMIT = 48 * 1024 * 1024


def swap(block, axis, mask):
    count = lax.axis_size(axis)
    return lax.ppermute(block, axis, [(i, i ^ mask) for i in range(count)])


def dot(left, right):
    return jnp.dot(left, right, preferred_element_type=F32)


def params(semantics=None):
    return pltpu.CompilerParams(vmem_limit_bytes=VMEM_LIMIT, dimension_semantics=semantics)


def cost(flops, nbytes):
    return pl.CostEstimate(flops=int(flops), bytes_accessed=int(nbytes), transcendentals=0)


def first_head(shape):
    return lax.broadcasted_iota(jnp.int32, shape, len(shape) - 1) < 64


def project_groups(tokens, w_qkv, incoming, scal, groups):
    total = sum(ROWS // SPANS[g] for g in groups)

    def body(scal_ref, tok_ref, w_ref, in_ref, keep_ref, send_ref, tmp_ref):
        which = pl.program_id(0)
        part = pl.program_id(1)
        tmp_ref[...] = dot(tok_ref[...], w_ref[...]).astype(BF)
        low = first_head((BLK, BLK))
        mine = scal_ref[32]

        def pick(src, slot, group, base):
            span = SPANS[group]
            for dst, pair in ((keep_ref, mine), (send_ref, 1 - mine)):
                col = pl.multiple_of(pair * BLK, BLK)
                off_a = scal_ref[group * 4 + 2 * pair]
                off_b = scal_ref[group * 4 + 2 * pair + 1]
                for r in range(8 // span):
                    row_a = pl.multiple_of((r * span + off_a) * BLK, BLK)
                    row_b = pl.multiple_of((r * span + off_b) * BLK, BLK)
                    blk_a = src[pl.ds(row_a, BLK), pl.ds(col, BLK)]
                    blk_b = src[pl.ds(row_b, BLK), pl.ds(col, BLK)]
                    dst[slot, pl.ds(base + r * BLK, BLK), :] = jnp.where(low, blk_a, blk_b)

        base = 0
        for n, group in enumerate(groups):

            @pl.when(which == n)
            def _(group=group, base=base):
                pick(tmp_ref, part, group, base)

                @pl.when(part == 0)
                def _():
                    pick(in_ref, 3, group, base)

            base += ROWS // SPANS[group]

    first = groups[0]
    out = jax.ShapeDtypeStruct((4, total, BLK), BF)
    return pl.pallas_call(
        body,
        grid_spec=pltpu.PrefetchScalarGridSpec(
            num_scalar_prefetch=1,
            grid=(len(groups), 3),
            in_specs=[
                pl.BlockSpec((ROWS, 1024), lambda i, j, s: (0, 0)),
                pl.BlockSpec((1024, 256), lambda i, j, s: (0, j * 4 + first + i)),
                pl.BlockSpec((ROWS, 256), lambda i, j, s: (0, first + i)),
            ],
            out_specs=[pl.BlockSpec((4, total, BLK), lambda i, j, s: (0, 0, 0))] * 2,
            scratch_shapes=[pltpu.VMEM((ROWS, 256), BF)],
        ),
        out_shape=[out, out],
        compiler_params=params(),
        cost_estimate=cost(len(groups) * 2 * 1024 * 1024 * 768, 6e6),
        name="project_kept",
    )(scal, tokens, w_qkv, incoming)


def project_dense(tokens, w_qkv):
    def body(tok_ref, w_ref, out_ref):
        res = dot(tok_ref[...], w_ref[...]).astype(BF)
        out_ref[0, 0] = res[:, :BLK]
        out_ref[0, 1] = res[:, BLK:]

    return pl.pallas_call(
        body,
        grid=(3,),
        in_specs=[
            pl.BlockSpec((ROWS, 1024), lambda j: (0, 0)),
            pl.BlockSpec((1024, 256), lambda j: (0, j * 4)),
        ],
        out_specs=pl.BlockSpec((1, 2, ROWS, BLK), lambda j: (j, 0, 0, 0)),
        out_shape=jax.ShapeDtypeStruct((3, 2, ROWS, BLK), BF),
        compiler_params=params(),
        cost_estimate=cost(2 * 1024 * 1024 * 768, 5e6),
        name="project_dense",
    )(tokens, w_qkv)


def pair_core(q_s, do_s, k_s, v_s, kt_s, vt_s, o_s, dq_s, dk_s, dv_s, q_rows):
    kt_s[...] = k_s[...].T
    vt_s[...] = v_s[...].T
    low_lane = first_head((CHUNK, BLK))
    low_row = lax.broadcasted_iota(jnp.int32, (BLK, CHUNK), 0) < 64
    zero = jnp.zeros((), BF)

    def step(c, _):
        rows = pl.ds(pl.multiple_of(c * CHUNK, CHUNK), CHUNK)
        q_c = q_s[rows, :] * jnp.asarray(0.125, BF)
        do_c = do_s[rows, :]
        q_t = q_c.T
        do_t = do_c.T
        outs, dqs = [], []
        d_v, d_k = None, None
        for a in range(2):
            mask = low_row if a == 0 else jnp.logical_not(low_row)
            lanes = low_lane if a == 0 else jnp.logical_not(low_lane)
            part = slice(a * 64, a * 64 + 64)
            scores = dot(k_s[...], jnp.where(mask, q_t, zero))
            top = jnp.max(scores, axis=0, keepdims=True)
            e = jnp.exp(scores - top)
            total = jnp.sum(e, axis=0, keepdims=True)
            prob = e * (1.0 / total)
            prob_b = prob.astype(BF)
            out_b = dot(vt_s[part, :], prob_b).astype(BF)
            delta = jnp.sum(
                do_t[part, :].astype(F32) * out_b.astype(F32), axis=0, keepdims=True
            )
            d_prob = dot(v_s[...], jnp.where(mask, do_t, zero))
            d_score = (prob * (d_prob - delta)).astype(BF)
            dqs.append(dot(kt_s[part, :], d_score) * 0.125)
            outs.append(out_b)
            dv_a = dot(prob_b, jnp.where(lanes, do_c, zero))
            dk_a = dot(d_score, jnp.where(lanes, q_c, zero))
            d_v = dv_a if d_v is None else d_v + dv_a
            d_k = dk_a if d_k is None else d_k + dk_a
        o_s[rows, :] = jnp.concatenate(outs, axis=0).T
        dq_s[rows, :] = jnp.concatenate(dqs, axis=0).T.astype(BF)

        @pl.when(c == 0)
        def _():
            dv_s[...] = d_v
            dk_s[...] = d_k

        @pl.when(c > 0)
        def _():
            dv_s[...] += d_v
            dk_s[...] += d_k

        return 0

    lax.fori_loop(0, q_rows // CHUNK, step, 0)


def attention_scratch(q_rows):
    return [
        pltpu.VMEM((q_rows, BLK), BF),
        pltpu.VMEM((q_rows, BLK), BF),
        pltpu.VMEM((ROWS, BLK), BF),
        pltpu.VMEM((ROWS, BLK), BF),
        pltpu.VMEM((BLK, ROWS), BF),
        pltpu.VMEM((BLK, ROWS), BF),
        pltpu.VMEM((q_rows, BLK), BF),
        pltpu.VMEM((q_rows, BLK), BF),
        pltpu.VMEM((ROWS, BLK), F32),
        pltpu.VMEM((ROWS, BLK), F32),
    ]


HEAD_FLOPS = 6 * 2 * 1024 * 1024 * 256


def attention_dense(qkv, incoming, pair):
    def body(qkv_ref, do_ref, out_ref, kt_s, vt_s, dk_s, dv_s):
        pair_core(
            qkv_ref.at[0, 0], do_ref, qkv_ref.at[1, 0], qkv_ref.at[2, 0], kt_s, vt_s,
            out_ref.at[0], out_ref.at[1], dk_s, dv_s, ROWS,
        )
        out_ref[2] = dk_s[...].astype(BF)
        out_ref[3] = dv_s[...].astype(BF)

    return pl.pallas_call(
        body,
        grid=(1,),
        in_specs=[
            pl.BlockSpec((3, 1, ROWS, BLK), lambda i: (0, pair, 0, 0)),
            pl.BlockSpec((ROWS, BLK), lambda i: (0, pair)),
        ],
        out_specs=pl.BlockSpec((4, ROWS, BLK), lambda i: (0, 0, 0)),
        out_shape=jax.ShapeDtypeStruct((4, ROWS, BLK), BF),
        scratch_shapes=attention_scratch(ROWS)[4:6] + attention_scratch(ROWS)[8:],
        compiler_params=params(),
        cost_estimate=cost(2 * HEAD_FLOPS, 2e6),
        name="attention_dense",
    )(qkv, incoming)


def attention_two(keep, recv):
    half = ROWS // 2

    def body(keep_ref, recv_ref, own_ref, back_ref, *scratch):
        q_s, do_s, k_s, v_s, kt_s, vt_s, o_s, dq_s, dk_s, dv_s = scratch
        for slot, dst in ((0, q_s), (1, k_s), (2, v_s), (3, do_s)):
            dst[:half, :] = keep_ref[slot]
            dst[half:, :] = recv_ref[slot]
        pair_core(q_s, do_s, k_s, v_s, kt_s, vt_s, o_s, dq_s, dk_s, dv_s, ROWS)
        for slot, src in ((0, o_s), (1, dq_s), (2, dk_s), (3, dv_s)):
            own_ref[slot] = src[:half, :].astype(BF)
            back_ref[slot] = src[half:, :].astype(BF)

    out = jax.ShapeDtypeStruct((4, half, BLK), BF)
    return pl.pallas_call(
        body,
        out_shape=[out, out],
        scratch_shapes=attention_scratch(ROWS),
        compiler_params=params(),
        cost_estimate=cost(2 * HEAD_FLOPS, 2e6),
        name="attention_two",
    )(keep, recv)


def attention_wide(keep, recv, from_2, from_4, from_6):
    def body(
        keep_ref, recv_ref, f2_ref, f4_ref, f6_ref,
        oq2_ref, loc2_ref, oq3_ref, loc3_ref, to2_ref, to4_ref, to6_ref, *scratch,
    ):
        q_s, do_s, k_s, v_s, kt_s, vt_s, o_s, dq_s, dk_s, dv_s = scratch
        for slot, dst in ((0, q_s), (3, do_s)):
            dst[0:256, :] = keep_ref[slot, 0:256, :]
            dst[256:512, :] = recv_ref[slot, 0:256, :]
        for n, dst in ((0, k_s), (1, v_s)):
            dst[0:256, :] = keep_ref[1 + n, 0:256, :]
            dst[256:512, :] = recv_ref[1 + n, 0:256, :]
            dst[512:, :] = f2_ref[n, 0:512, :]
        pair_core(q_s, do_s, k_s, v_s, kt_s, vt_s, o_s, dq_s, dk_s, dv_s, 512)
        oq2_ref[0] = o_s[...]
        oq2_ref[1] = dq_s[...]
        for n, src in ((0, dk_s), (1, dv_s)):
            loc2_ref[n] = src[:512, :]
            to2_ref[n, 0:512, :] = src[512:, :].astype(BF)
        for slot, dst in ((0, q_s), (3, do_s)):
            dst[0:128, :] = keep_ref[slot, 256:384, :]
            dst[128:256, :] = recv_ref[slot, 256:384, :]
        for n, dst in ((0, k_s), (1, v_s)):
            dst[0:128, :] = keep_ref[1 + n, 256:384, :]
            dst[128:256, :] = recv_ref[1 + n, 256:384, :]
            dst[256:512, :] = f2_ref[n, 512:768, :]
            dst[512:768, :] = f4_ref[n]
            dst[768:, :] = f6_ref[n]
        pair_core(q_s, do_s, k_s, v_s, kt_s, vt_s, o_s, dq_s, dk_s, dv_s, 256)
        oq3_ref[0] = o_s[:256, :]
        oq3_ref[1] = dq_s[:256, :]
        for n, src in ((0, dk_s), (1, dv_s)):
            loc3_ref[n] = src[:256, :]
            to2_ref[n, 512:768, :] = src[256:512, :].astype(BF)
            to4_ref[n] = src[512:768, :].astype(BF)
            to6_ref[n] = src[768:, :].astype(BF)

    shapes = [
        ((2, 512, BLK), BF), ((2, 512, BLK), F32), ((2, 256, BLK), BF), ((2, 256, BLK), F32),
        ((2, 768, BLK), BF), ((2, 256, BLK), BF), ((2, 256, BLK), BF),
    ]
    return pl.pallas_call(
        body,
        out_shape=[jax.ShapeDtypeStruct(s, d) for s, d in shapes],
        scratch_shapes=attention_scratch(512),
        compiler_params=params(),
        cost_estimate=cost(1.5 * HEAD_FLOPS, 2e6),
        name="attention_wide",
    )(keep, recv, from_2, from_4, from_6)


def combine_wide(oq2, loc2, oq3, loc3, ret2, ret4, ret6):
    def body(oq2_ref, loc2_ref, oq3_ref, loc3_ref, r2_ref, r4_ref, r6_ref, own_ref, back_ref):
        for dst, at2, at3 in ((own_ref, 0, 0), (back_ref, 256, 128)):
            two = slice(at2, at2 + 256)
            three = slice(at3, at3 + 128)
            for n in range(2):
                dst[n, 0:256, :] = oq2_ref[n, two, :]
                dst[n, 256:384, :] = oq3_ref[n, three, :]
                dst[2 + n, 0:256, :] = (loc2_ref[n, two, :] + r2_ref[n, two, :].astype(F32)).astype(BF)
                far = r4_ref[n, three, :].astype(F32) + r6_ref[n, three, :].astype(F32)
                near = r2_ref[n, 512 + at3 : 640 + at3, :].astype(F32)
                dst[2 + n, 256:384, :] = (loc3_ref[n, three, :] + near + far).astype(BF)

    out = jax.ShapeDtypeStruct((4, 384, BLK), BF)
    return pl.pallas_call(
        body,
        out_shape=[out, out],
        compiler_params=params(),
        cost_estimate=cost(1e6, 2e6),
        name="combine_wide",
    )(oq2, loc2, oq3, loc3, ret2, ret4, ret6)


def block_mask(block, span, off_a, off_b, low):
    here = block % span
    keep_a = jnp.where(off_a == here, 1, 0)
    keep_b = jnp.where(off_b == here, 1, 0)
    return jnp.where(low, keep_a, keep_b) == 1


def weight_grad(tokens, tokens_other, mine, other, scal, group, base, table):
    span = SPANS[group]

    def body(scal_ref, tok_ref, tok2_ref, mine_ref, other_ref, send_ref, keep_ref, g_s):
        i = pl.program_id(0)

        @pl.when(i == 0)
        def _():
            low = first_head((BLK, BLK))
            pair = scal_ref[33]
            for n, src in ((0, mine_ref), (1, other_ref)):
                off_a = scal_ref[n * 16 + group * 4 + 2 * pair]
                off_b = scal_ref[n * 16 + group * 4 + 2 * pair + 1]
                for block in range(8):
                    mask = block_mask(block, span, off_a, off_b, low)
                    row = base + (block // span) * BLK
                    for part in range(3):
                        val = src[part, row : row + BLK, :]
                        g_s[n * ROWS + block * BLK : n * ROWS + block * BLK + BLK,
                            part * BLK : part * BLK + BLK] = jnp.where(mask, val, jnp.zeros((), BF))

        over_rows = (((0,), (0,)), ((), ()))
        res = lax.dot_general(tok_ref[...], g_s[:ROWS, :], over_rows, preferred_element_type=F32)
        res += lax.dot_general(tok2_ref[...], g_s[ROWS:, :], over_rows, preferred_element_type=F32)

        @pl.when(i < 2)
        def _():
            send_ref[0] = res.astype(BF)

        @pl.when(i >= 2)
        def _():
            keep_ref[0] = res

    slab = mine.shape[1]
    return pl.pallas_call(
        body,
        grid_spec=pltpu.PrefetchScalarGridSpec(
            num_scalar_prefetch=1,
            grid=(4,),
            in_specs=[
                pl.BlockSpec((ROWS, 256), lambda i, s: (0, s[table + i])),
                pl.BlockSpec((ROWS, 256), lambda i, s: (0, s[table + i])),
                pl.BlockSpec((3, slab, BLK), lambda i, s: (0, 0, 0)),
                pl.BlockSpec((3, slab, BLK), lambda i, s: (0, 0, 0)),
            ],
            out_specs=[
                pl.BlockSpec((1, 256, 384), lambda i, s: (jnp.minimum(i, 1), 0, 0)),
                pl.BlockSpec((1, 256, 384), lambda i, s: (jnp.maximum(i - 2, 0), 0, 0)),
            ],
            scratch_shapes=[pltpu.VMEM((2 * ROWS, 384), BF)],
        ),
        out_shape=[
            jax.ShapeDtypeStruct((2, 256, 384), BF),
            jax.ShapeDtypeStruct((2, 256, 384), F32),
        ],
        compiler_params=params(),
        cost_estimate=cost(2 * 1024 * 2048 * 384, 5e6),
        name="weight_grad",
    )(scal, tokens, tokens_other, mine, other)


def token_grad(w_qkv, scal, dense, one, wide):
    def body(scal_ref, w_ref, d0_ref, d1_ref, o1_ref, r1_ref, ow_ref, rw_ref, att_ref, dx_ref, g_s):
        i = pl.program_id(0)

        @pl.when(i == 0)
        def _():
            low = first_head((BLK, BLK))
            zero = jnp.zeros((), BF)
            mine = scal_ref[32]
            for part in range(4):
                for pair, src in ((0, d0_ref), (1, d1_ref)):
                    if part == 0:
                        att_ref[:, pair * BLK : pair * BLK + BLK] = src[0]
                    else:
                        col = (part - 1) * 1024 + pair * BLK
                        g_s[:, col : col + BLK] = src[part]
            for group, base, own, ret in ((1, 0, o1_ref, r1_ref), (2, 0, ow_ref, rw_ref), (3, 256, ow_ref, rw_ref)):
                span = SPANS[group]
                for src, pair in ((own, mine), (ret, 1 - mine)):
                    off_a = scal_ref[group * 4 + 2 * pair]
                    off_b = scal_ref[group * 4 + 2 * pair + 1]
                    for block in range(8):
                        mask = block_mask(block, span, off_a, off_b, low)
                        row = base + (block // span) * BLK
                        rows = slice(block * BLK, block * BLK + BLK)
                        for part in range(4):
                            val = jnp.where(mask, src[part, row : row + BLK, :], zero)
                            col = group * 256 + pair * BLK
                            if part == 0:
                                att_ref[rows, pl.ds(pl.multiple_of(col, BLK), BLK)] = val
                            else:
                                col = col + (part - 1) * 1024
                                g_s[rows, pl.ds(pl.multiple_of(col, BLK), BLK)] = val

        dx_ref[...] = lax.dot_general(
            g_s[...], w_ref[...], (((1,), (1,)), ((), ())), preferred_element_type=F32
        ).astype(BF)

    def whole(shape):
        return pl.BlockSpec(shape, lambda i, s: (0,) * len(shape))

    out = jax.ShapeDtypeStruct((ROWS, 1024), BF)
    return pl.pallas_call(
        body,
        grid_spec=pltpu.PrefetchScalarGridSpec(
            num_scalar_prefetch=1,
            grid=(4,),
            in_specs=[
                pl.BlockSpec((256, 3072), lambda i, s: (i, 0)),
                whole((4, ROWS, BLK)), whole((4, ROWS, BLK)),
                whole((4, 512, BLK)), whole((4, 512, BLK)),
                whole((4, 384, BLK)), whole((4, 384, BLK)),
            ],
            out_specs=[
                pl.BlockSpec((ROWS, 1024), lambda i, s: (0, 0)),
                pl.BlockSpec((ROWS, 256), lambda i, s: (0, i)),
            ],
            scratch_shapes=[pltpu.VMEM((ROWS, 3072), BF)],
        ),
        out_shape=[out, out],
        compiler_params=params(),
        cost_estimate=cost(2 * 1024 * 1024 * 3072, 12e6),
        name="token_grad",
    )(scal, w_qkv, dense[0], dense[1], one[0], one[1], wide[0], wide[1])


def per_device(tokens, w_qkv, offsets, d_attended):
    inputs = tokens[0]
    incoming = d_attended[0]
    seq = lax.axis_index("seq")
    core = lax.axis_index("dp") & 1
    b0, b1, b2 = seq & 1, (seq >> 1) & 1, (seq >> 2) & 1
    gray = b1 ^ b2

    def start_p(j, f):
        return 2 * j + (f ^ j)

    def start_q(j, f):
        return 2 * f + j

    tail = [b0, core]
    tail += [start_p(0, 1 - gray), start_p(1, 1 - gray), start_p(0, gray), start_p(1, gray)]
    tail += [start_q(0, 1 - b2), start_q(1, 1 - b2), start_q(0, b2), start_q(1, b2)]
    tail = [jnp.asarray(t, jnp.int32) for t in tail]
    row = offsets[0]
    row_other = swap(row, "dp", 1)
    scal_own = jnp.concatenate([row, row, jnp.stack(tail)])
    scal = jnp.concatenate([row, row_other, jnp.stack(tail)])
    table_p, table_q = 34, 38

    inputs_other = swap(inputs, "dp", 1)

    keep_w, send_w = project_groups(inputs, w_qkv, incoming, scal_own, (2, 3))
    recv_w = swap(send_w, "seq", 1)
    keep_1, send_1 = project_groups(inputs, w_qkv, incoming, scal_own, (1,))
    recv_1 = swap(send_1, "seq", 1)
    qkv_0 = project_dense(inputs, w_qkv)

    kv_3 = jnp.concatenate([keep_w[1:3, 256:], recv_w[1:3, 256:]], axis=1)
    kv_2 = jnp.concatenate([keep_w[1:3, :256], recv_w[1:3, :256], kv_3], axis=1)
    from_2 = swap(kv_2, "seq", 2)
    from_4 = swap(kv_3, "seq", 4)
    from_6 = swap(kv_3, "seq", 6)

    dense = [attention_dense(qkv_0, incoming, pair) for pair in range(2)]

    oq2, loc2, oq3, loc3, to2, to4, to6 = attention_wide(keep_w, recv_w, from_2, from_4, from_6)
    ret2 = swap(to2, "seq", 2)
    ret4 = swap(to4, "seq", 4)
    ret6 = swap(to6, "seq", 6)
    own_1, back_1 = attention_two(keep_1, recv_1)
    ret_1 = swap(back_1, "seq", 1)
    own_w, back_w = combine_wide(oq2, loc2, oq3, loc3, ret2, ret4, ret6)
    ret_w = swap(back_w, "seq", 1)

    def halves(first, second, same):
        mine = jnp.where(same, first[1:], second[1:])
        other = jnp.where(same, second[1:], first[1:])
        return mine, swap(other, "dp", 1)

    def reduce_seq(send, keep, kind):
        near, far, bit = (2, 6, b2) if kind == 0 else (6, 2, b1)
        total = keep + swap(send, "seq", near).astype(F32)
        leave = jnp.where(bit == 0, total[1], total[0]).astype(BF)
        stay = jnp.where(bit == 0, total[0], total[1])
        return stay + swap(leave, "seq", far).astype(F32)

    def finish(parts):
        total = jnp.concatenate(parts, axis=1)
        leave = jnp.where(b0 == 0, total[128:], total[:128]).astype(BF)
        stay = jnp.where(b0 == 0, total[:128], total[128:])
        total = stay + swap(leave, "seq", 1).astype(F32)
        for mask in (2, 6, 8):
            half = total.astype(BF)
            total = half.astype(F32) + swap(half, "dp", mask).astype(F32)
        return total

    mine_0, other_0 = halves(dense[0], dense[1], core == 0)
    send, keep = weight_grad(inputs, inputs_other, mine_0, other_0, scal, 0, 0, table_p)
    part_0 = reduce_seq(send, keep, 0)
    mine_1, other_1 = halves(own_1, ret_1, core == b0)
    send, keep = weight_grad(inputs, inputs_other, mine_1, other_1, scal, 1, 0, table_q)
    part_1 = reduce_seq(send, keep, 1)
    done_01 = finish([part_0, part_1])
    mine_w, other_w = halves(own_w, ret_w, core == b0)
    send, keep = weight_grad(inputs, inputs_other, mine_w, other_w, scal, 2, 0, table_p)
    part_2 = reduce_seq(send, keep, 0)
    send, keep = weight_grad(inputs, inputs_other, mine_w, other_w, scal, 3, 256, table_q)
    part_3 = reduce_seq(send, keep, 1)
    done_23 = finish([part_2, part_3])

    attended, d_inputs = token_grad(w_qkv, scal_own, dense, (own_1, ret_1), (own_w, ret_w))

    done = jnp.concatenate([done_01, done_23], axis=1)
    done_other = swap(done, "dp", 1)
    low = jnp.where(core == 0, done, done_other).reshape(128, 4, 3, 128)
    high = jnp.where(core == 0, done_other, done).reshape(128, 4, 3, 128)
    both = jnp.stack([low, high], axis=3)
    d_weights = jnp.transpose(both, (0, 2, 1, 3, 4)).reshape(128, 3072)
    return (attended[None], d_inputs[None], d_weights)


def solution(mesh):
    placed = (P("dp", "seq", None), P(), P("dp", None), P("dp", "seq", None))
    return jax.shard_map(
        per_device,
        mesh=mesh,
        in_specs=placed,
        out_specs=(P("dp", "seq", None), P("dp", "seq", None), P("seq", None)),
        check_vma=False,
    )
```

```python
import jax
import jax.numpy as jnp
from jax import lax
from jax.experimental import pallas as pl
from jax.experimental.pallas import tpu as pltpu
from jax.sharding import PartitionSpec as P

BLK = 128
ROWS = 1024
BF = jnp.bfloat16
F32 = jnp.float32
SPANS = (1, 2, 4, 8)
VMEM_LIMIT = 48 * 1024 * 1024


def swap(block, axis, mask):
    count = lax.axis_size(axis)
    return lax.ppermute(block, axis, [(i, i ^ mask) for i in range(count)])


def dot(left, right):
    return jnp.dot(left, right, preferred_element_type=F32)


def params(semantics=None):
    return pltpu.CompilerParams(vmem_limit_bytes=VMEM_LIMIT, dimension_semantics=semantics)


def cost(flops, nbytes):
    return pl.CostEstimate(flops=int(flops), bytes_accessed=int(nbytes), transcendentals=0)


def with_order(body, n_in, n_dep):
    def ordered(*refs):
        return body(*refs[:n_in], *refs[n_in + n_dep :])

    return ordered


ANY = pl.BlockSpec(memory_space=pl.ANY)
WHOLE = pl.BlockSpec(memory_space=pltpu.VMEM)


def first_head(shape):
    return lax.broadcasted_iota(jnp.int32, shape, len(shape) - 1) < 64


def turn(block):
    return pltpu.roll(block.astype(F32), 64, axis=1).astype(block.dtype)


def head_columns(query, key, value, head):
    low = first_head(query.shape)
    if head == 0:
        return jnp.concatenate([jnp.where(low, query, turn(key)), value], axis=1)
    return jnp.concatenate([jnp.where(low, turn(query), key), value], axis=1)


def project_groups(tokens, w_qkv, incoming, scal, groups, deps=()):
    total = sum(ROWS // SPANS[g] for g in groups)

    def body(scal_ref, tok_ref, wq_ref, wk_ref, wv_ref, in_ref, keep_ref, send_ref, x_s):
        which = pl.program_id(0)
        mine = scal_ref[32]

        def work(group, base):
            span = SPANS[group]
            rows = ROWS // span
            low = first_head((rows, BLK))
            low_blk = first_head((BLK, BLK))
            for dst, pair in ((keep_ref, mine), (send_ref, 1 - mine)):
                lanes = pl.ds(pl.multiple_of(pair * BLK, BLK), BLK)
                offs = [scal_ref[group * 4 + 2 * pair + head] for head in range(2)]
                res = []
                for head in range(2):
                    for r in range(8 // span):
                        row = pl.multiple_of((r * span + offs[head]) * BLK, BLK)
                        x_s[r * BLK : r * BLK + BLK, :] = tok_ref[pl.ds(row, BLK), :]
                    cols = head_columns(wq_ref[:, lanes], wk_ref[:, lanes], wv_ref[:, lanes], head)
                    res.append(dot(x_s[:rows, :], cols))
                here = slice(base, base + rows)
                front = [r[:, :BLK] for r in res]
                back = [r[:, BLK:] for r in res]
                dst[0, here, :] = jnp.where(low, front[0], turn(front[1])).astype(BF)
                dst[1, here, :] = jnp.where(low, turn(front[0]), front[1]).astype(BF)
                dst[2, here, :] = jnp.where(low, back[0], back[1]).astype(BF)
                for r in range(8 // span):
                    blks = []
                    for head in range(2):
                        row = pl.multiple_of((r * span + offs[head]) * BLK, BLK)
                        blks.append(in_ref[pl.ds(row, BLK), lanes])
                    dst[3, base + r * BLK : base + r * BLK + BLK, :] = jnp.where(low_blk, blks[0], blks[1])

        base = 0
        for n, group in enumerate(groups):

            @pl.when(which == n)
            def _(group=group, base=base):
                work(group, base)

            base += ROWS // SPANS[group]

    first = groups[0]
    out = jax.ShapeDtypeStruct((4, total, BLK), BF)
    return pl.pallas_call(
        with_order(body, 6, len(deps)),
        grid_spec=pltpu.PrefetchScalarGridSpec(
            num_scalar_prefetch=1,
            grid=(len(groups),),
            in_specs=[WHOLE]
            + [
                pl.BlockSpec((1024, 256), lambda i, s, part=part: (0, part * 4 + first + i))
                for part in range(3)
            ]
            + [pl.BlockSpec((ROWS, 256), lambda i, s: (0, first + i))]
            + [ANY] * len(deps),
            out_specs=[pl.BlockSpec((4, total, BLK), lambda i, s: (0, 0, 0))] * 2,
            scratch_shapes=[pltpu.VMEM((ROWS // SPANS[first], 1024), BF)],
        ),
        out_shape=[out, out],
        compiler_params=params(),
        cost_estimate=cost(len(groups) * 2 * 1024 * 1024 * 768, 6e6),
        name="project_kept",
    )(scal, tokens, w_qkv, w_qkv, w_qkv, incoming, *deps)


def project_dense(tokens, w_qkv, deps=()):
    def body(tok_ref, w_ref, out_ref):
        res = dot(tok_ref[...], w_ref[...]).astype(BF)
        out_ref[0, 0] = res[:, :BLK]
        out_ref[0, 1] = res[:, BLK:]

    return pl.pallas_call(
        with_order(body, 2, len(deps)),
        grid=(3,),
        in_specs=[
            WHOLE,
            pl.BlockSpec((1024, 256), lambda j: (0, j * 4)),
        ]
        + [ANY] * len(deps),
        out_specs=pl.BlockSpec((1, 2, ROWS, BLK), lambda j: (j, 0, 0, 0)),
        out_shape=jax.ShapeDtypeStruct((3, 2, ROWS, BLK), BF),
        compiler_params=params(),
        cost_estimate=cost(2 * 1024 * 1024 * 768, 5e6),
        name="project_dense",
    )(tokens, w_qkv, *deps)


def pair_core(q_s, do_s, k_s, v_s, kt_s, vt_s, o_s, dq_s, dk_s, dv_s, q_rows):
    kt_s[...] = k_s[...].T
    vt_s[...] = v_s[...].T
    low_lane = first_head((q_rows, BLK))
    low_row = lax.broadcasted_iota(jnp.int32, (BLK, q_rows), 0) < 64
    zero = jnp.zeros((), BF)

    q_c = q_s[:q_rows, :] * jnp.asarray(0.125, BF)
    do_c = do_s[:q_rows, :]
    q_t = q_c.T
    do_t = do_c.T
    outs, dqs, probs, d_scores, dos, qs = [], [], [], [], [], []
    for a in range(2):
        mask = low_row if a == 0 else jnp.logical_not(low_row)
        lanes = low_lane if a == 0 else jnp.logical_not(low_lane)
        part = slice(a * 64, a * 64 + 64)
        scores = dot(k_s[...], jnp.where(mask, q_t, zero))
        top = jnp.max(scores, axis=0, keepdims=True)
        e = jnp.exp(scores - top)
        total = jnp.sum(e, axis=0, keepdims=True)
        prob = e * (1.0 / total)
        prob_b = prob.astype(BF)
        out_b = dot(vt_s[part, :], prob_b).astype(BF)
        delta = jnp.sum(do_t[part, :].astype(F32) * out_b.astype(F32), axis=0, keepdims=True)
        d_prob = dot(v_s[...], jnp.where(mask, do_t, zero))
        d_score = (prob * (d_prob - delta)).astype(BF)
        dqs.append(dot(kt_s[part, :], d_score) * 0.125)
        outs.append(out_b)
        probs.append(prob_b)
        d_scores.append(d_score)
        dos.append(jnp.where(lanes, do_c, zero))
        qs.append(jnp.where(lanes, q_c, zero))
    dv_s[...] = dot(jnp.concatenate(probs, axis=1), jnp.concatenate(dos, axis=0))
    dk_s[...] = dot(jnp.concatenate(d_scores, axis=1), jnp.concatenate(qs, axis=0))
    o_s[:q_rows, :] = jnp.concatenate(outs, axis=0).T
    dq_s[:q_rows, :] = jnp.concatenate(dqs, axis=0).T.astype(BF)


def attention_scratch(q_rows):
    return [
        pltpu.VMEM((q_rows, BLK), BF),
        pltpu.VMEM((q_rows, BLK), BF),
        pltpu.VMEM((ROWS, BLK), BF),
        pltpu.VMEM((ROWS, BLK), BF),
        pltpu.VMEM((BLK, ROWS), BF),
        pltpu.VMEM((BLK, ROWS), BF),
        pltpu.VMEM((q_rows, BLK), BF),
        pltpu.VMEM((q_rows, BLK), BF),
        pltpu.VMEM((ROWS, BLK), F32),
        pltpu.VMEM((ROWS, BLK), F32),
    ]


HEAD_FLOPS = 6 * 2 * 1024 * 1024 * 256


def attention_dense(qkv, incoming, pair, deps=()):
    def body(qkv_ref, do_ref, out_ref, kt_s, vt_s, dk_s, dv_s):
        pair_core(
            qkv_ref.at[0, 0], do_ref, qkv_ref.at[1, 0], qkv_ref.at[2, 0], kt_s, vt_s,
            out_ref.at[0], out_ref.at[1], dk_s, dv_s, ROWS,
        )
        out_ref[2] = dk_s[...].astype(BF)
        out_ref[3] = dv_s[...].astype(BF)

    return pl.pallas_call(
        with_order(body, 2, len(deps)),
        grid=(1,),
        in_specs=[
            pl.BlockSpec((3, 1, ROWS, BLK), lambda i: (0, pair, 0, 0)),
            pl.BlockSpec((ROWS, BLK), lambda i: (0, pair)),
        ]
        + [ANY] * len(deps),
        out_specs=pl.BlockSpec((4, ROWS, BLK), lambda i: (0, 0, 0)),
        out_shape=jax.ShapeDtypeStruct((4, ROWS, BLK), BF),
        scratch_shapes=attention_scratch(ROWS)[4:6] + attention_scratch(ROWS)[8:],
        compiler_params=params(),
        cost_estimate=cost(2 * HEAD_FLOPS, 2e6),
        name="attention_dense",
    )(qkv, incoming, *deps)


def attention_two(keep, recv, deps=()):
    half = ROWS // 2

    def body(keep_ref, recv_ref, own_ref, back_ref, *scratch):
        q_s, do_s, k_s, v_s, kt_s, vt_s, o_s, dq_s, dk_s, dv_s = scratch
        for slot, dst in ((0, q_s), (1, k_s), (2, v_s), (3, do_s)):
            dst[:half, :] = keep_ref[slot]
            dst[half:, :] = recv_ref[slot]
        pair_core(q_s, do_s, k_s, v_s, kt_s, vt_s, o_s, dq_s, dk_s, dv_s, ROWS)
        for slot, src in ((0, o_s), (1, dq_s), (2, dk_s), (3, dv_s)):
            own_ref[slot] = src[:half, :].astype(BF)
            back_ref[slot] = src[half:, :].astype(BF)

    out = jax.ShapeDtypeStruct((4, half, BLK), BF)
    return pl.pallas_call(
        with_order(body, 2, len(deps)),
        in_specs=[WHOLE] * 2 + [ANY] * len(deps),
        out_shape=[out, out],
        scratch_shapes=attention_scratch(ROWS),
        compiler_params=params(),
        cost_estimate=cost(2 * HEAD_FLOPS, 2e6),
        name="attention_two",
    )(keep, recv, *deps)


def pack_pairs(keep, recv, deps=()):
    def body(keep_ref, recv_ref, all_ref, three_ref):
        for n in range(2):
            for at, src in ((0, keep_ref), (1, recv_ref)):
                two = src[1 + n, 0:256, :]
                three = src[1 + n, 256:384, :]
                all_ref[n, at * 256 : at * 256 + 256, :] = two
                all_ref[n, 512 + at * 128 : 640 + at * 128, :] = three
                three_ref[n, at * 128 : at * 128 + 128, :] = three

    return pl.pallas_call(
        with_order(body, 2, len(deps)),
        in_specs=[WHOLE] * 2 + [ANY] * len(deps),
        out_shape=[jax.ShapeDtypeStruct((2, n, BLK), BF) for n in (768, 256)],
        compiler_params=params(),
        cost_estimate=cost(1e6, 1e4),
        name="pack_pairs",
    )(keep, recv, *deps)


def attention_wide(keep, recv, from_2, from_4, from_6, deps=()):
    def body(
        keep_ref, recv_ref, f2_ref, f4_ref, f6_ref,
        oq2_ref, loc2_ref, oq3_ref, loc3_ref, to2_ref, to4_ref, to6_ref, *scratch,
    ):
        q_s, do_s, k_s, v_s, kt_s, vt_s, o_s, dq_s, dk_s, dv_s = scratch
        for slot, dst in ((0, q_s), (3, do_s)):
            dst[0:256, :] = keep_ref[slot, 0:256, :]
            dst[256:512, :] = recv_ref[slot, 0:256, :]
        for n, dst in ((0, k_s), (1, v_s)):
            dst[0:256, :] = keep_ref[1 + n, 0:256, :]
            dst[256:512, :] = recv_ref[1 + n, 0:256, :]
            dst[512:, :] = f2_ref[n, 0:512, :]
        pair_core(q_s, do_s, k_s, v_s, kt_s, vt_s, o_s, dq_s, dk_s, dv_s, 512)
        oq2_ref[0] = o_s[...]
        oq2_ref[1] = dq_s[...]
        for n, src in ((0, dk_s), (1, dv_s)):
            loc2_ref[n] = src[:512, :]
            to2_ref[n, 0:512, :] = src[512:, :].astype(BF)
        for slot, dst in ((0, q_s), (3, do_s)):
            dst[0:128, :] = keep_ref[slot, 256:384, :]
            dst[128:256, :] = recv_ref[slot, 256:384, :]
        for n, dst in ((0, k_s), (1, v_s)):
            dst[0:128, :] = keep_ref[1 + n, 256:384, :]
            dst[128:256, :] = recv_ref[1 + n, 256:384, :]
            dst[256:512, :] = f2_ref[n, 512:768, :]
            dst[512:768, :] = f4_ref[n]
            dst[768:, :] = f6_ref[n]
        pair_core(q_s, do_s, k_s, v_s, kt_s, vt_s, o_s, dq_s, dk_s, dv_s, 256)
        oq3_ref[0] = o_s[:256, :]
        oq3_ref[1] = dq_s[:256, :]
        for n, src in ((0, dk_s), (1, dv_s)):
            loc3_ref[n] = src[:256, :]
            to2_ref[n, 512:768, :] = src[256:512, :].astype(BF)
            to4_ref[n] = src[512:768, :].astype(BF)
            to6_ref[n] = src[768:, :].astype(BF)

    shapes = [
        ((2, 512, BLK), BF), ((2, 512, BLK), F32), ((2, 256, BLK), BF), ((2, 256, BLK), F32),
        ((2, 768, BLK), BF), ((2, 256, BLK), BF), ((2, 256, BLK), BF),
    ]
    return pl.pallas_call(
        with_order(body, 5, len(deps)),
        in_specs=[WHOLE] * 5 + [ANY] * len(deps),
        out_shape=[jax.ShapeDtypeStruct(s, d) for s, d in shapes],
        scratch_shapes=attention_scratch(512),
        compiler_params=params(),
        cost_estimate=cost(1.5 * HEAD_FLOPS, 2e6),
        name="attention_wide",
    )(keep, recv, from_2, from_4, from_6, *deps)


def combine_wide(oq2, loc2, oq3, loc3, ret2, ret4, ret6, deps=()):
    def body(oq2_ref, loc2_ref, oq3_ref, loc3_ref, r2_ref, r4_ref, r6_ref, own_ref, back_ref):
        for dst, at2, at3 in ((own_ref, 0, 0), (back_ref, 256, 128)):
            two = slice(at2, at2 + 256)
            three = slice(at3, at3 + 128)
            for n in range(2):
                dst[n, 0:256, :] = oq2_ref[n, two, :]
                dst[n, 256:384, :] = oq3_ref[n, three, :]
                dst[2 + n, 0:256, :] = (loc2_ref[n, two, :] + r2_ref[n, two, :].astype(F32)).astype(BF)
                far = r4_ref[n, three, :].astype(F32) + r6_ref[n, three, :].astype(F32)
                near = r2_ref[n, 512 + at3 : 640 + at3, :].astype(F32)
                dst[2 + n, 256:384, :] = (loc3_ref[n, three, :] + near + far).astype(BF)

    out = jax.ShapeDtypeStruct((4, 384, BLK), BF)
    return pl.pallas_call(
        with_order(body, 7, len(deps)),
        in_specs=[WHOLE] * 7 + [ANY] * len(deps),
        out_shape=[out, out],
        compiler_params=params(),
        cost_estimate=cost(1e6, 1e4),
        name="combine_wide",
    )(oq2, loc2, oq3, loc3, ret2, ret4, ret6, *deps)


def choose_pairs(scal, sources, weight, deps=()):
    slabs = [src[0].shape[1] for src in sources]
    total = sum(slabs)

    def body(scal_ref, *refs):
        mine_ref, other_ref = refs[-2:]
        core = scal_ref[33]
        base = 0
        for n, slab in enumerate(slabs):
            first, second = refs[2 * n : 2 * n + 2]
            same = core == (0 if slab == ROWS else scal_ref[32])
            here = slice(base, base + slab)

            def copy(one, two, here=here):
                for part in range(3):
                    mine_ref[part, here, :] = one[1 + part]
                    other_ref[part, here, :] = two[1 + part]

            pl.when(same)(lambda first=first, second=second, copy=copy: copy(first, second))
            pl.when(jnp.logical_not(same))(
                lambda first=first, second=second, copy=copy: copy(second, first)
            )
            base += slab

    flat = [x for source in sources for x in source]
    out = jax.ShapeDtypeStruct((3, total, BLK), BF)
    return pl.pallas_call(
        with_order(body, 1 + len(flat), len(deps)),
        in_specs=[pl.BlockSpec(memory_space=pltpu.SMEM)] + [WHOLE] * len(flat) + [ANY] * len(deps),
        out_shape=[out, out],
        compiler_params=params(),
        cost_estimate=cost(weight, 1e4),
        name="choose_pairs",
    )(scal, *flat, *deps)


def block_mask(block, span, off_a, off_b, low):
    here = block % span
    keep_a = jnp.where(off_a == here, 1, 0)
    keep_b = jnp.where(off_b == here, 1, 0)
    return jnp.where(low, keep_a, keep_b) == 1


def weight_grad(tokens, tokens_other, scal, groups, mine, other, weight, deps=()):
    count = len(groups) * 192
    tables = (34, 38)

    def body(scal_ref, tok_ref, tok2_ref, mine_ref, other_ref, *refs):
        outs = refs[:4]
        l_s, x_s = refs[4:]
        core = scal_ref[33]
        base = 0
        for at, group in enumerate(groups):
            span = SPANS[group]
            rows = ROWS // span
            for n, src in ((0, mine_ref), (1, other_ref)):
                to = slice(n * rows, n * rows + rows)
                for part in range(3):
                    val = src[part, base : base + rows, :].T
                    l_s[part * 64 : part * 64 + 64, to] = val[:64]
                    l_s[192 + part * 64 : 256 + part * 64, to] = val[64:]
            base += rows
            for head in range(2):
                left = l_s.at[head * 192 : head * 192 + 192, :]
                starts = [pl.multiple_of(scal_ref[tables[head] + j] * 256, 256) for j in range(4)]
                if span > 1:
                    for n, tok in ((0, tok_ref), (1, tok2_ref)):
                        off = scal_ref[n * 16 + group * 4 + 2 * core + head]
                        for r in range(8 // span):
                            row = pl.multiple_of((r * span + off) * BLK, BLK)
                            to = n * rows + r * BLK
                            for j in range(4):
                                x_s[to : to + BLK, j * 256 : j * 256 + 256] = tok[
                                    pl.ds(row, BLK), pl.ds(starts[j], 256)
                                ]
                for j in range(4):
                    if span > 1:
                        res = dot(left[:, : 2 * rows], x_s[: 2 * rows, j * 256 : j * 256 + 256])
                    else:
                        lanes = pl.ds(starts[j], 256)
                        res = dot(left[:, :ROWS], tok_ref[:, lanes])
                        res += dot(left[:, ROWS:], tok2_ref[:, lanes])
                    to = slice(at * 192, at * 192 + 192)
                    if j < 2:
                        outs[2 * head][j, to, :] = res.astype(BF)
                    else:
                        outs[2 * head + 1][j - 2, to, :] = res

    smem = pl.BlockSpec(memory_space=pltpu.SMEM)
    return pl.pallas_call(
        with_order(body, 5, len(deps)),
        in_specs=[smem] + [WHOLE] * 4 + [ANY] * len(deps),
        out_shape=[jax.ShapeDtypeStruct((2, count, 256), d) for d in (BF, F32, BF, F32)],
        scratch_shapes=[
            pltpu.VMEM((384, 2 * ROWS), BF),
            pltpu.VMEM((ROWS, 1024), BF),
        ],
        compiler_params=params(),
        cost_estimate=cost(weight, 1e4),
        name="weight_grad",
    )(scal, tokens, tokens_other, mine, other, *deps)


def fold_x(scal, keep_p, recv_p, keep_q, recv_q, deps=()):
    rows = keep_p.shape[1]

    def body(scal_ref, kp, rp, kq, rq, stay_p, leave_p, stay_q, leave_q):
        for bit, keep, recv, stay, leave in (
            (scal_ref[43], kp, rp, stay_p, leave_p),
            (scal_ref[42], kq, rq, stay_q, leave_q),
        ):
            stay[...] = keep[bit] + recv[bit].astype(F32)
            leave[...] = (keep[1 - bit] + recv[1 - bit].astype(F32)).astype(BF)

    return pl.pallas_call(
        with_order(body, 5, len(deps)),
        in_specs=[pl.BlockSpec(memory_space=pltpu.SMEM)] + [WHOLE] * 4 + [ANY] * len(deps),
        out_shape=[jax.ShapeDtypeStruct((rows, 256), d) for d in (F32, BF, F32, BF)],
        compiler_params=params(),
        cost_estimate=cost(1e6, 1e4),
        name="fold_x",
    )(scal, keep_p, recv_p, keep_q, recv_q, *deps)


def fold_y(scal, stay_p, recv_p, stay_q, recv_q, deps=()):
    rows = stay_p.shape[0]

    def body(scal_ref, sp, rp, sq, rq, stay, leave):
        bit = scal_ref[32]
        here = pl.ds(pl.multiple_of(bit * BLK, BLK), BLK)
        there = pl.ds(pl.multiple_of((1 - bit) * BLK, BLK), BLK)
        for at, own, recv in ((0, sp, rp), (rows, sq, rq)):
            stay[at : at + rows, :] = own[:, here] + recv[:, here].astype(F32)
            leave[at : at + rows, :] = (own[:, there] + recv[:, there].astype(F32)).astype(BF)

    return pl.pallas_call(
        with_order(body, 5, len(deps)),
        in_specs=[pl.BlockSpec(memory_space=pltpu.SMEM)] + [WHOLE] * 4 + [ANY] * len(deps),
        out_shape=[jax.ShapeDtypeStruct((2 * rows, BLK), d) for d in (F32, BF)],
        compiler_params=params(),
        cost_estimate=cost(1e6, 1e4),
        name="fold_y",
    )(scal, stay_p, recv_p, stay_q, recv_q, *deps)


def over_columns(left, right):
    return lax.dot_general(left, right, (((1,), (1,)), ((), ())), preferred_element_type=F32)


def token_grad(w_qkv, scal, dense, one, wide, half, before=None, deps=()):
    def body(scal_ref, w_ref, d0_ref, d1_ref, o1_ref, r1_ref, ow_ref, rw_ref, *refs):
        acc = refs[-1]
        flag_ref = refs[-2]
        dx_ref = refs[-3]
        flag_ref[...] = jnp.zeros_like(flag_ref)
        mine = scal_ref[32]
        total = None
        for part in range(3):
            left = jnp.concatenate([d0_ref[1 + part], d1_ref[1 + part]], axis=1)
            term = over_columns(left, w_ref[:, part * 1024 : part * 1024 + 256])
            total = term if total is None else total + term
        acc[...] = total
        for group, base, own, ret in (
            (1, 0, o1_ref, r1_ref), (2, 0, ow_ref, rw_ref), (3, 256, ow_ref, rw_ref),
        ):
            span = SPANS[group]
            rows = ROWS // span
            low = first_head((rows, BLK))
            zero = jnp.zeros((), BF)
            for src, pair in ((own, mine), (ret, 1 - mine)):
                weights = []
                for part in range(3):
                    col = pl.multiple_of(part * 1024 + group * 256 + pair * BLK, BLK)
                    weights.append(w_ref[:, pl.ds(col, BLK)])
                d_q, d_k, d_v = [src[1 + part, base : base + rows, :] for part in range(3)]
                for head in range(2):
                    if head == 0:
                        d_v_head = jnp.where(low, d_v, zero)
                    else:
                        d_v_head = jnp.where(low, zero, d_v)
                    left = head_columns(d_q, d_k, d_v_head, head)
                    res = over_columns(left, head_columns(*weights, head))
                    off = scal_ref[group * 4 + 2 * pair + head]
                    for r in range(8 // span):
                        at = pl.ds(pl.multiple_of((r * span + off) * BLK, BLK), BLK)
                        acc[at, :] += res[r * BLK : r * BLK + BLK, :]
        dx_ref[...] = acc[...].astype(BF)
        if half == 0:
            att_ref = refs[-4]
            low = first_head((BLK, BLK))
            att_ref[:, 0:BLK] = d0_ref[0]
            att_ref[:, BLK : 2 * BLK] = d1_ref[0]
            for group, base, own, ret in (
                (1, 0, o1_ref, r1_ref), (2, 0, ow_ref, rw_ref), (3, 256, ow_ref, rw_ref),
            ):
                span = SPANS[group]
                for src, pair in ((own, mine), (ret, 1 - mine)):
                    off_a = scal_ref[group * 4 + 2 * pair]
                    off_b = scal_ref[group * 4 + 2 * pair + 1]
                    lanes = pl.ds(pl.multiple_of(group * 256 + pair * BLK, BLK), BLK)
                    for block in range(8):
                        mask = block_mask(block, span, off_a, off_b, low)
                        row = base + (block // span) * BLK
                        val = src[0, row : row + BLK, :]
                        rows = slice(block * BLK, block * BLK + BLK)
                        att_ref[rows, lanes] = jnp.where(mask, val, jnp.zeros((), BF))

    out = jax.ShapeDtypeStruct((ROWS, 1024), BF)
    dx_spec = pl.BlockSpec((ROWS, 512), lambda i, s: (0, half))
    given = () if before is None else (before,)
    outs = [out] if half else [out, out]
    outs += [jax.ShapeDtypeStruct((8, BLK), F32)]
    flag_spec = pl.BlockSpec((8, BLK), lambda i, s: (0, 0))
    return pl.pallas_call(
        with_order(body, 8, len(given) + len(deps)),
        grid_spec=pltpu.PrefetchScalarGridSpec(
            num_scalar_prefetch=1,
            grid=(1,),
            in_specs=[pl.BlockSpec((512, 3072), lambda i, s: (half, 0))]
            + [WHOLE] * 6
            + [ANY] * (len(given) + len(deps)),
            out_specs=([] if half else [pl.BlockSpec((ROWS, 1024), lambda i, s: (0, 0))]) + [dx_spec, flag_spec],
            scratch_shapes=[pltpu.VMEM((ROWS, 512), F32)],
        ),
        out_shape=outs,
        input_output_aliases={8: 0} if half else {},
        compiler_params=params(),
        cost_estimate=cost(1e6, 1e4),
        name="token_grad",
    )(scal, w_qkv, dense[0], dense[1], one[0], one[1], wide[0], wide[1], *given, *deps)


def place_weights(scal, parts, groups_of):
    def body(scal_ref, *refs):
        out = refs[-1]
        core = scal_ref[33]
        at = 0
        for groups in groups_of:
            for pair in (core, 1 - core):
                for n, group in enumerate(groups):
                    for part in range(3):
                        row = n * 192 + part * 64
                        far = len(groups) * 192 + row
                        val = jnp.concatenate(
                            [refs[at][row : row + 64, :], refs[at][far : far + 64, :]], axis=0
                        )
                        col = pl.multiple_of(part * 1024 + group * 256 + pair * BLK, BLK)
                        out[:, pl.ds(col, BLK)] = val.T
                at += 1

    return pl.pallas_call(
        body,
        in_specs=[pl.BlockSpec(memory_space=pltpu.SMEM)] + [WHOLE] * len(parts),
        out_shape=jax.ShapeDtypeStruct((BLK, 3072), F32),
        compiler_params=params(),
        cost_estimate=cost(1e6, 1e4),
        name="place_weights",
    )(scal, *parts)


def per_device(tokens, w_qkv, offsets, d_attended):
    inputs = tokens[0]
    incoming = d_attended[0]
    seq = lax.axis_index("seq")
    core = lax.axis_index("dp") & 1
    b0, b1, b2 = seq & 1, (seq >> 1) & 1, (seq >> 2) & 1
    gray = b1 ^ b2

    def start_p(j, f):
        return 2 * j + (f ^ j)

    def start_q(j, f):
        return 2 * f + j

    tail = [b0, core]
    tail += [start_p(0, 1 - gray), start_p(1, 1 - gray), start_p(0, gray), start_p(1, gray)]
    tail += [start_q(0, 1 - b2), start_q(1, 1 - b2), start_q(0, b2), start_q(1, b2)]
    tail += [b1, b2]
    tail = [jnp.asarray(t, jnp.int32) for t in tail]
    row = offsets[0]
    row_other = swap(row, "dp", 1)
    scal_own = jnp.concatenate([row, row, jnp.stack(tail)])
    scal = jnp.concatenate([row, row_other, jnp.stack(tail)])
    table_p, table_q = 34, 38

    inputs_other = swap(inputs, "dp", 1)

    keep_w, send_w = project_groups(inputs, w_qkv, incoming, scal_own, (2, 3))
    recv_w = swap(send_w, "seq", 1)
    keep_1, send_1 = project_groups(inputs, w_qkv, incoming, scal_own, (1,), (keep_w, inputs_other[:8, :BLK], scal))
    recv_1 = swap(send_1, "seq", 1)
    qkv_0 = project_dense(inputs, w_qkv, (keep_1,))

    kv_2, kv_3 = pack_pairs(keep_w, recv_w, (qkv_0,))
    from_2 = swap(kv_2, "seq", 2)
    from_4 = swap(kv_3, "seq", 4)
    from_6 = swap(kv_3, "seq", 6)

    dense_0 = attention_dense(qkv_0, incoming, 0, (kv_3,))
    wide = attention_wide(keep_w, recv_w, from_2, from_4, from_6, (dense_0,))
    oq2, loc2, oq3, loc3, to2, to4, to6 = wide
    ret2 = swap(to2, "seq", 2)
    ret4 = swap(to4, "seq", 4)
    ret6 = swap(to6, "seq", 6)
    own_1, back_1 = attention_two(keep_1, recv_1, (oq2,))
    ret_1 = swap(back_1, "seq", 1)
    own_w, back_w = combine_wide(oq2, loc2, oq3, loc3, ret2, ret4, ret6, (own_1,))
    ret_w = swap(back_w, "seq", 1)
    dense_1 = attention_dense(qkv_0, incoming, 1, (own_w,))
    dense = (dense_0, dense_1)
    one = (own_1, ret_1)
    far = (own_w, ret_w)

    mine_m, other_m = choose_pairs(scal_own, (dense, one), 1e6)
    core_m = swap(other_m, "dp", 1)
    mine_f, other_f = choose_pairs(scal_own, (far,), 10e9, (mine_m,))
    core_f = swap(other_f, "dp", 1)
    grads_m = weight_grad(inputs, inputs_other, scal, (0, 1), mine_m, core_m, 10e9, (mine_f,))
    grads_f = weight_grad(inputs, inputs_other, scal, (2, 3), mine_f, core_f, 1e6, (grads_m[0],))

    def first_swap(grads):
        send_p, keep_p, send_q, keep_q = grads
        return keep_p, swap(send_p, "seq", 2), keep_q, swap(send_q, "seq", 6)

    def second_swap(folded):
        stay_p, leave_p, stay_q, leave_q = folded
        return stay_p, swap(leave_p, "seq", 6), stay_q, swap(leave_q, "seq", 2)

    def reduce_rest(stay, leave):
        total = stay + swap(leave, "seq", 1).astype(F32)
        for mask in (2, 6):
            half = total.astype(BF)
            total = half.astype(F32) + swap(half, "dp", mask).astype(F32)
        total = total + swap(total, "dp", 8)
        return [total, swap(total, "dp", 1)]

    attended, d_half, flag = token_grad(w_qkv, scal, dense, one, far, 0, None, (grads_f[0],))
    folded_m = fold_x(scal, *first_swap(grads_m), (flag,))
    d_inputs, flag = token_grad(w_qkv, scal, dense, one, far, 1, d_half, (folded_m[0],))
    folded_f = fold_x(scal, *first_swap(grads_f), (flag,))
    rest_m = fold_y(scal, *second_swap(folded_m), (folded_f[0],))
    rest_f = fold_y(scal, *second_swap(folded_f), (rest_m[0],))
    parts = reduce_rest(*rest_m) + reduce_rest(*rest_f)
    d_weights = place_weights(scal, parts, ((0, 1), (2, 3)))
    return (attended[None], d_inputs[None], d_weights)


def solution(mesh):
    placed = (P("dp", "seq", None), P(), P("dp", None), P("dp", "seq", None))
    return jax.shard_map(
        per_device,
        mesh=mesh,
        in_specs=placed,
        out_specs=(P("dp", "seq", None), P("dp", "seq", None), P("seq", None)),
        check_vma=False,
    )
```

```python
import jax
import jax.numpy as jnp
from jax import lax
from jax.experimental import pallas as pl
from jax.experimental.pallas import tpu as pltpu
from jax.sharding import PartitionSpec as P

BLK = 128
ROWS = 1024
BF = jnp.bfloat16
F32 = jnp.float32
SPANS = (1, 2, 4, 8)
VMEM_LIMIT = 48 * 1024 * 1024


def swap(block, axis, mask):
    count = lax.axis_size(axis)
    return lax.ppermute(block, axis, [(i, i ^ mask) for i in range(count)])


def dot(left, right):
    return jnp.dot(left, right, preferred_element_type=F32)


def params(semantics=None):
    return pltpu.CompilerParams(vmem_limit_bytes=VMEM_LIMIT, dimension_semantics=semantics)


def cost(flops, nbytes):
    return pl.CostEstimate(flops=int(flops), bytes_accessed=int(nbytes), transcendentals=0)


def with_order(body, n_in, n_dep):
    def ordered(*refs):
        return body(*refs[:n_in], *refs[n_in + n_dep :])

    return ordered


ANY = pl.BlockSpec(memory_space=pl.ANY)
WHOLE = pl.BlockSpec(memory_space=pltpu.VMEM)


def first_head(shape):
    return lax.broadcasted_iota(jnp.int32, shape, len(shape) - 1) < 64


def turn(block):
    return pltpu.roll(block.astype(F32), 64, axis=1).astype(block.dtype)


def head_columns(query, key, value, head):
    low = first_head(query.shape)
    if head == 0:
        return jnp.concatenate([jnp.where(low, query, turn(key)), value], axis=1)
    return jnp.concatenate([jnp.where(low, turn(query), key), value], axis=1)


def project_groups(tokens, w_qkv, incoming, scal, groups, deps=()):
    total = sum(ROWS // SPANS[g] for g in groups)
    wide = len(groups) == 2


    def pick_incoming(in_ref, dst, base, group, pair, offs, first_col):
        low = first_head((BLK, BLK))
        span = SPANS[group]
        lanes = pl.ds(pl.multiple_of(first_col + pair * BLK, BLK), BLK)
        for r in range(8 // span):
            blks = []
            for head in range(2):
                row = pl.multiple_of((r * span + offs[head]) * BLK, BLK)
                blks.append(in_ref[pl.ds(row, BLK), lanes])
            dst[base + r * BLK : base + r * BLK + BLK, :] = jnp.where(low, blks[0], blks[1])

    def body(scal_ref, tok_ref, wq_ref, wk_ref, wv_ref, *refs):
        which = pl.program_id(0)
        mine = scal_ref[32]
        x_s = refs[-1]
        if wide:
            in_ref, keep_ref, send_ref, keep1_ref, send1_ref, zero_ref = refs[:6]

            @pl.when(which == 0)
            def _():
                zero_ref[0] = in_ref[:, 0:BLK]
                zero_ref[1] = in_ref[:, BLK : 2 * BLK]

            @pl.when(which == 1)
            def _():
                for dst, pair in ((keep1_ref, mine), (send1_ref, 1 - mine)):
                    offs = [scal_ref[4 + 2 * pair + head] for head in range(2)]
                    pick_incoming(in_ref, dst, 0, 1, pair, offs, 256)
        else:
            given, keep_ref, send_ref = refs[:2], refs[2], refs[3]

        def work(group, base):
            span = SPANS[group]
            rows = ROWS // span
            low = first_head((rows, BLK))
            for n, (dst, pair) in enumerate(((keep_ref, mine), (send_ref, 1 - mine))):
                lanes = pl.ds(pl.multiple_of(pair * BLK, BLK), BLK)
                offs = [scal_ref[group * 4 + 2 * pair + head] for head in range(2)]
                res = []
                for head in range(2):
                    for r in range(8 // span):
                        row = pl.multiple_of((r * span + offs[head]) * BLK, BLK)
                        x_s[r * BLK : r * BLK + BLK, :] = tok_ref[pl.ds(row, BLK), :]
                    cols = head_columns(wq_ref[:, lanes], wk_ref[:, lanes], wv_ref[:, lanes], head)
                    res.append(dot(x_s[:rows, :], cols))
                here = slice(base, base + rows)
                front = [r[:, :BLK] for r in res]
                back = [r[:, BLK:] for r in res]
                dst[0, here, :] = jnp.where(low, front[0], turn(front[1])).astype(BF)
                dst[1, here, :] = jnp.where(low, turn(front[0]), front[1]).astype(BF)
                dst[2, here, :] = jnp.where(low, back[0], back[1]).astype(BF)
                if wide:
                    pick_incoming(in_ref, dst.at[3], base, group, pair, offs, group * 256)
                else:
                    dst[3] = given[n][...]

        base = 0
        for n, group in enumerate(groups):

            @pl.when(which == n)
            def _(group=group, base=base):
                work(group, base)

            base += ROWS // SPANS[group]

    first = groups[0]
    half = ROWS // 2
    shapes = [(4, total, BLK)] * 2
    if wide:
        shapes += [(half, BLK)] * 2 + [(2, ROWS, BLK)]
    given = (incoming,) if wide else incoming
    return pl.pallas_call(
        with_order(body, 5 + len(given), len(deps)),
        grid_spec=pltpu.PrefetchScalarGridSpec(
            num_scalar_prefetch=1,
            grid=(len(groups),),
            in_specs=[WHOLE]
            + [
                pl.BlockSpec((1024, 256), lambda i, s, part=part: (0, part * 4 + first + i))
                for part in range(3)
            ]
            + [WHOLE] * len(given)
            + [ANY] * len(deps),
            out_specs=[
                pl.BlockSpec(shape, lambda i, s, n=len(shape): (0,) * n) for shape in shapes
            ],
            scratch_shapes=[pltpu.VMEM((ROWS // SPANS[first], 1024), BF)],
        ),
        out_shape=[jax.ShapeDtypeStruct(shape, BF) for shape in shapes],
        compiler_params=params(),
        cost_estimate=cost(len(groups) * 2 * 1024 * 1024 * 768, 6e6),
        name="project_kept",
    )(scal, tokens, w_qkv, w_qkv, w_qkv, *given, *deps)


def project_dense(tokens, w_qkv, deps=()):
    def body(tok_ref, w_ref, out_ref):
        res = dot(tok_ref[...], w_ref[...]).astype(BF)
        out_ref[0, 0] = res[:, :BLK]
        out_ref[0, 1] = res[:, BLK:]

    return pl.pallas_call(
        with_order(body, 2, len(deps)),
        grid=(3,),
        in_specs=[
            WHOLE,
            pl.BlockSpec((1024, 256), lambda j: (0, j * 4)),
        ]
        + [ANY] * len(deps),
        out_specs=pl.BlockSpec((1, 2, ROWS, BLK), lambda j: (j, 0, 0, 0)),
        out_shape=jax.ShapeDtypeStruct((3, 2, ROWS, BLK), BF),
        compiler_params=params(),
        cost_estimate=cost(2 * 1024 * 1024 * 768, 5e6),
        name="project_dense",
    )(tokens, w_qkv, *deps)


def pair_core(q_s, do_s, k_s, v_s, kt_s, vt_s, o_s, dq_s, dk_s, dv_s, q_rows):
    kt_s[...] = k_s[...].T
    vt_s[...] = v_s[...].T
    low_lane = first_head((q_rows, BLK))
    low_row = lax.broadcasted_iota(jnp.int32, (BLK, q_rows), 0) < 64
    zero = jnp.zeros((), BF)

    q_c = q_s[:q_rows, :] * jnp.asarray(0.125, BF)
    do_c = do_s[:q_rows, :]
    q_t = q_c.T
    do_t = do_c.T
    outs, dqs, probs, d_scores, dos, qs = [], [], [], [], [], []
    for a in range(2):
        mask = low_row if a == 0 else jnp.logical_not(low_row)
        lanes = low_lane if a == 0 else jnp.logical_not(low_lane)
        part = slice(a * 64, a * 64 + 64)
        scores = dot(k_s[...], jnp.where(mask, q_t, zero))
        top = jnp.max(scores, axis=0, keepdims=True)
        e = jnp.exp(scores - top)
        total = jnp.sum(e, axis=0, keepdims=True)
        prob = e * (1.0 / total)
        prob_b = prob.astype(BF)
        out_b = dot(vt_s[part, :], prob_b).astype(BF)
        delta = jnp.sum(do_t[part, :].astype(F32) * out_b.astype(F32), axis=0, keepdims=True)
        d_prob = dot(v_s[...], jnp.where(mask, do_t, zero))
        d_score = (prob * (d_prob - delta)).astype(BF)
        dqs.append(dot(kt_s[part, :], d_score) * 0.125)
        outs.append(out_b)
        probs.append(prob_b)
        d_scores.append(d_score)
        dos.append(jnp.where(lanes, do_c, zero))
        qs.append(jnp.where(lanes, q_c, zero))
    dv_s[...] = dot(jnp.concatenate(probs, axis=1), jnp.concatenate(dos, axis=0))
    dk_s[...] = dot(jnp.concatenate(d_scores, axis=1), jnp.concatenate(qs, axis=0))
    o_s[:q_rows, :] = jnp.concatenate(outs, axis=0).T
    dq_s[:q_rows, :] = jnp.concatenate(dqs, axis=0).T.astype(BF)


def attention_scratch(q_rows):
    return [
        pltpu.VMEM((q_rows, BLK), BF),
        pltpu.VMEM((q_rows, BLK), BF),
        pltpu.VMEM((ROWS, BLK), BF),
        pltpu.VMEM((ROWS, BLK), BF),
        pltpu.VMEM((BLK, ROWS), BF),
        pltpu.VMEM((BLK, ROWS), BF),
        pltpu.VMEM((q_rows, BLK), BF),
        pltpu.VMEM((q_rows, BLK), BF),
        pltpu.VMEM((ROWS, BLK), F32),
        pltpu.VMEM((ROWS, BLK), F32),
    ]


HEAD_FLOPS = 6 * 2 * 1024 * 1024 * 256


def attention_dense(qkv, incoming, pair, deps=()):
    def body(qkv_ref, do_ref, out_ref, kt_s, vt_s, dk_s, dv_s):
        pair_core(
            qkv_ref.at[0, 0], do_ref.at[0], qkv_ref.at[1, 0], qkv_ref.at[2, 0], kt_s, vt_s,
            out_ref.at[0], out_ref.at[1], dk_s, dv_s, ROWS,
        )
        out_ref[2] = dk_s[...].astype(BF)
        out_ref[3] = dv_s[...].astype(BF)

    return pl.pallas_call(
        with_order(body, 2, len(deps)),
        grid=(1,),
        in_specs=[
            pl.BlockSpec((3, 1, ROWS, BLK), lambda i: (0, pair, 0, 0)),
            pl.BlockSpec((1, ROWS, BLK), lambda i: (pair, 0, 0)),
        ]
        + [ANY] * len(deps),
        out_specs=pl.BlockSpec((4, ROWS, BLK), lambda i: (0, 0, 0)),
        out_shape=jax.ShapeDtypeStruct((4, ROWS, BLK), BF),
        scratch_shapes=attention_scratch(ROWS)[4:6] + attention_scratch(ROWS)[8:],
        compiler_params=params(),
        cost_estimate=cost(2 * HEAD_FLOPS, 2e6),
        name="attention_dense",
    )(qkv, incoming, *deps)


def attention_two(keep, recv, deps=()):
    half = ROWS // 2

    def body(keep_ref, recv_ref, own_ref, back_ref, out_ref, *scratch):
        q_s, do_s, k_s, v_s, kt_s, vt_s, o_s, dq_s, dk_s, dv_s = scratch
        for slot, dst in ((0, q_s), (1, k_s), (2, v_s), (3, do_s)):
            dst[:half, :] = keep_ref[slot]
            dst[half:, :] = recv_ref[slot]
        pair_core(q_s, do_s, k_s, v_s, kt_s, vt_s, o_s, dq_s, dk_s, dv_s, ROWS)
        for slot, src in ((0, dq_s), (1, dk_s), (2, dv_s)):
            own_ref[slot] = src[:half, :].astype(BF)
            back_ref[slot] = src[half:, :].astype(BF)
        out_ref[0] = o_s[:half, :]
        out_ref[1] = o_s[half:, :]

    out = jax.ShapeDtypeStruct((3, half, BLK), BF)
    return pl.pallas_call(
        with_order(body, 2, len(deps)),
        in_specs=[WHOLE] * 2 + [ANY] * len(deps),
        out_shape=[out, out, jax.ShapeDtypeStruct((2, half, BLK), BF)],
        scratch_shapes=attention_scratch(ROWS),
        compiler_params=params(),
        cost_estimate=cost(2 * HEAD_FLOPS, 2e6),
        name="attention_two",
    )(keep, recv, *deps)


def pack_pairs(keep, recv, deps=()):
    def body(keep_ref, recv_ref, all_ref, three_ref):
        for n in range(2):
            for at, src in ((0, keep_ref), (1, recv_ref)):
                two = src[1 + n, 0:256, :]
                three = src[1 + n, 256:384, :]
                all_ref[n, at * 256 : at * 256 + 256, :] = two
                all_ref[n, 512 + at * 128 : 640 + at * 128, :] = three
                three_ref[n, at * 128 : at * 128 + 128, :] = three

    return pl.pallas_call(
        with_order(body, 2, len(deps)),
        in_specs=[WHOLE] * 2 + [ANY] * len(deps),
        out_shape=[jax.ShapeDtypeStruct((2, n, BLK), BF) for n in (768, 256)],
        compiler_params=params(),
        cost_estimate=cost(1e6, 1e4),
        name="pack_pairs",
    )(keep, recv, *deps)


def attention_wide(keep, recv, from_2, from_4, from_6, deps=()):
    def body(
        keep_ref, recv_ref, f2_ref, f4_ref, f6_ref,
        oq2_ref, loc2_ref, oq3_ref, loc3_ref, to2_ref, to4_ref, to6_ref, *scratch,
    ):
        q_s, do_s, k_s, v_s, kt_s, vt_s, o_s, dq_s, dk_s, dv_s = scratch
        for slot, dst in ((0, q_s), (3, do_s)):
            dst[0:256, :] = keep_ref[slot, 0:256, :]
            dst[256:512, :] = recv_ref[slot, 0:256, :]
        for n, dst in ((0, k_s), (1, v_s)):
            dst[0:256, :] = keep_ref[1 + n, 0:256, :]
            dst[256:512, :] = recv_ref[1 + n, 0:256, :]
            dst[512:, :] = f2_ref[n, 0:512, :]
        pair_core(q_s, do_s, k_s, v_s, kt_s, vt_s, o_s, dq_s, dk_s, dv_s, 512)
        oq2_ref[0] = o_s[...]
        oq2_ref[1] = dq_s[...]
        for n, src in ((0, dk_s), (1, dv_s)):
            loc2_ref[n] = src[:512, :]
            to2_ref[n, 0:512, :] = src[512:, :].astype(BF)
        for slot, dst in ((0, q_s), (3, do_s)):
            dst[0:128, :] = keep_ref[slot, 256:384, :]
            dst[128:256, :] = recv_ref[slot, 256:384, :]
        for n, dst in ((0, k_s), (1, v_s)):
            dst[0:128, :] = keep_ref[1 + n, 256:384, :]
            dst[128:256, :] = recv_ref[1 + n, 256:384, :]
            dst[256:512, :] = f2_ref[n, 512:768, :]
            dst[512:768, :] = f4_ref[n]
            dst[768:, :] = f6_ref[n]
        pair_core(q_s, do_s, k_s, v_s, kt_s, vt_s, o_s, dq_s, dk_s, dv_s, 256)
        oq3_ref[0] = o_s[:256, :]
        oq3_ref[1] = dq_s[:256, :]
        for n, src in ((0, dk_s), (1, dv_s)):
            loc3_ref[n] = src[:256, :]
            to2_ref[n, 512:768, :] = src[256:512, :].astype(BF)
            to4_ref[n] = src[512:768, :].astype(BF)
            to6_ref[n] = src[768:, :].astype(BF)

    shapes = [
        ((2, 512, BLK), BF), ((2, 512, BLK), F32), ((2, 256, BLK), BF), ((2, 256, BLK), F32),
        ((2, 768, BLK), BF), ((2, 256, BLK), BF), ((2, 256, BLK), BF),
    ]
    return pl.pallas_call(
        with_order(body, 5, len(deps)),
        in_specs=[WHOLE] * 5 + [ANY] * len(deps),
        out_shape=[jax.ShapeDtypeStruct(s, d) for s, d in shapes],
        scratch_shapes=attention_scratch(512),
        compiler_params=params(),
        cost_estimate=cost(1.5 * HEAD_FLOPS, 2e6),
        name="attention_wide",
    )(keep, recv, from_2, from_4, from_6, *deps)


def combine_wide(oq2, loc2, oq3, loc3, ret2, ret4, ret6, out_one, deps=()):
    def body(oq2_ref, loc2_ref, oq3_ref, loc3_ref, r2_ref, r4_ref, r6_ref, one_ref, *refs):
        own_ref, back_ref, out_own, out_back = refs
        for n, (dst, out, at2, at3) in enumerate(
            ((own_ref, out_own, 0, 0), (back_ref, out_back, 256, 128))
        ):
            two = slice(at2, at2 + 256)
            three = slice(at3, at3 + 128)
            out[0:512, :] = one_ref[n]
            out[512:768, :] = oq2_ref[0, two, :]
            out[768:896, :] = oq3_ref[0, three, :]
            dst[0, 0:256, :] = oq2_ref[1, two, :]
            dst[0, 256:384, :] = oq3_ref[1, three, :]
            for n in range(2):
                dst[1 + n, 0:256, :] = (loc2_ref[n, two, :] + r2_ref[n, two, :].astype(F32)).astype(BF)
                far = r4_ref[n, three, :].astype(F32) + r6_ref[n, three, :].astype(F32)
                near = r2_ref[n, 512 + at3 : 640 + at3, :].astype(F32)
                dst[1 + n, 256:384, :] = (loc3_ref[n, three, :] + near + far).astype(BF)

    shapes = [(3, 384, BLK)] * 2 + [(896, BLK)] * 2
    return pl.pallas_call(
        with_order(body, 8, len(deps)),
        in_specs=[WHOLE] * 8 + [ANY] * len(deps),
        out_shape=[jax.ShapeDtypeStruct(shape, BF) for shape in shapes],
        compiler_params=params(),
        cost_estimate=cost(1e6, 1e4),
        name="combine_wide",
    )(oq2, loc2, oq3, loc3, ret2, ret4, ret6, out_one, *deps)


def choose_pairs(scal, sources, weight, deps=()):
    slabs = [src[0].shape[1] for src in sources]
    total = sum(slabs)

    def body(scal_ref, *refs):
        mine_ref, other_ref = refs[-2:]
        core = scal_ref[33]
        base = 0
        for n, slab in enumerate(slabs):
            first, second = refs[2 * n : 2 * n + 2]
            same = core == (0 if slab == ROWS else scal_ref[32])
            here = slice(base, base + slab)

            def copy(one, two, here=here, slot=1 if slab == ROWS else 0):
                for part in range(3):
                    mine_ref[part, here, :] = one[slot + part]
                    other_ref[part, here, :] = two[slot + part]

            pl.when(same)(lambda first=first, second=second, copy=copy: copy(first, second))
            pl.when(jnp.logical_not(same))(
                lambda first=first, second=second, copy=copy: copy(second, first)
            )
            base += slab

    flat = [x for source in sources for x in source]
    out = jax.ShapeDtypeStruct((3, total, BLK), BF)
    return pl.pallas_call(
        with_order(body, 1 + len(flat), len(deps)),
        in_specs=[pl.BlockSpec(memory_space=pltpu.SMEM)] + [WHOLE] * len(flat) + [ANY] * len(deps),
        out_shape=[out, out],
        compiler_params=params(),
        cost_estimate=cost(weight, 1e4),
        name="choose_pairs",
    )(scal, *flat, *deps)


def block_mask(block, span, off_a, off_b, low):
    here = block % span
    keep_a = jnp.where(off_a == here, 1, 0)
    keep_b = jnp.where(off_b == here, 1, 0)
    return jnp.where(low, keep_a, keep_b) == 1


def weight_grad(tokens, tokens_other, scal, groups, mine, other, weight, deps=()):
    count = len(groups) * 192
    tables = (34, 38)

    def body(scal_ref, tok_ref, tok2_ref, mine_ref, other_ref, *refs):
        outs = refs[:4]
        l_s, x_s = refs[4:]
        core = scal_ref[33]
        base = 0
        for at, group in enumerate(groups):
            span = SPANS[group]
            rows = ROWS // span
            for n, src in ((0, mine_ref), (1, other_ref)):
                to = slice(n * rows, n * rows + rows)
                for part in range(3):
                    val = src[part, base : base + rows, :].T
                    l_s[part * 64 : part * 64 + 64, to] = val[:64]
                    l_s[192 + part * 64 : 256 + part * 64, to] = val[64:]
            base += rows
            for head in range(2):
                left = l_s.at[head * 192 : head * 192 + 192, :]
                starts = [pl.multiple_of(scal_ref[tables[head] + j] * 256, 256) for j in range(4)]
                if span > 1:
                    for n, tok in ((0, tok_ref), (1, tok2_ref)):
                        off = scal_ref[n * 16 + group * 4 + 2 * core + head]
                        for r in range(8 // span):
                            row = pl.multiple_of((r * span + off) * BLK, BLK)
                            to = n * rows + r * BLK
                            for j in range(4):
                                x_s[to : to + BLK, j * 256 : j * 256 + 256] = tok[
                                    pl.ds(row, BLK), pl.ds(starts[j], 256)
                                ]
                for j in range(4):
                    if span > 1:
                        res = dot(left[:, : 2 * rows], x_s[: 2 * rows, j * 256 : j * 256 + 256])
                    else:
                        lanes = pl.ds(starts[j], 256)
                        res = dot(left[:, :ROWS], tok_ref[:, lanes])
                        res += dot(left[:, ROWS:], tok2_ref[:, lanes])
                    to = slice(at * 192, at * 192 + 192)
                    if j < 2:
                        outs[2 * head][j, to, :] = res.astype(BF)
                    else:
                        outs[2 * head + 1][j - 2, to, :] = res

    smem = pl.BlockSpec(memory_space=pltpu.SMEM)
    return pl.pallas_call(
        with_order(body, 5, len(deps)),
        in_specs=[smem] + [WHOLE] * 4 + [ANY] * len(deps),
        out_shape=[jax.ShapeDtypeStruct((2, count, 256), d) for d in (BF, F32, BF, F32)],
        scratch_shapes=[
            pltpu.VMEM((384, 2 * ROWS), BF),
            pltpu.VMEM((ROWS, 1024), BF),
        ],
        compiler_params=params(),
        cost_estimate=cost(weight, 1e4),
        name="weight_grad",
    )(scal, tokens, tokens_other, mine, other, *deps)


def fold_x(scal, keep_p, recv_p, keep_q, recv_q, deps=()):
    rows = keep_p.shape[1]

    def body(scal_ref, kp, rp, kq, rq, stay_p, leave_p, stay_q, leave_q):
        for bit, keep, recv, stay, leave in (
            (scal_ref[43], kp, rp, stay_p, leave_p),
            (scal_ref[42], kq, rq, stay_q, leave_q),
        ):
            stay[...] = keep[bit] + recv[bit].astype(F32)
            leave[...] = (keep[1 - bit] + recv[1 - bit].astype(F32)).astype(BF)

    return pl.pallas_call(
        with_order(body, 5, len(deps)),
        in_specs=[pl.BlockSpec(memory_space=pltpu.SMEM)] + [WHOLE] * 4 + [ANY] * len(deps),
        out_shape=[jax.ShapeDtypeStruct((rows, 256), d) for d in (F32, BF, F32, BF)],
        compiler_params=params(),
        cost_estimate=cost(1e6, 1e4),
        name="fold_x",
    )(scal, keep_p, recv_p, keep_q, recv_q, *deps)


def fold_y(scal, stay_p, recv_p, stay_q, recv_q, deps=()):
    rows = stay_p.shape[0]

    def body(scal_ref, sp, rp, sq, rq, stay, leave):
        bit = scal_ref[32]
        here = pl.ds(pl.multiple_of(bit * BLK, BLK), BLK)
        there = pl.ds(pl.multiple_of((1 - bit) * BLK, BLK), BLK)
        for at, own, recv in ((0, sp, rp), (rows, sq, rq)):
            stay[at : at + rows, :] = own[:, here] + recv[:, here].astype(F32)
            leave[at : at + rows, :] = (own[:, there] + recv[:, there].astype(F32)).astype(BF)

    return pl.pallas_call(
        with_order(body, 5, len(deps)),
        in_specs=[pl.BlockSpec(memory_space=pltpu.SMEM)] + [WHOLE] * 4 + [ANY] * len(deps),
        out_shape=[jax.ShapeDtypeStruct((2 * rows, BLK), d) for d in (F32, BF)],
        compiler_params=params(),
        cost_estimate=cost(1e6, 1e4),
        name="fold_y",
    )(scal, stay_p, recv_p, stay_q, recv_q, *deps)


def over_columns(left, right):
    return lax.dot_general(left, right, (((1,), (1,)), ((), ())), preferred_element_type=F32)


def token_grad(w_qkv, scal, dense, one, wide, width, piece, before=None, outs_of=(), deps=()):
    start = before is None
    last = len(outs_of) > 0

    def body(scal_ref, w_ref, d0_ref, d1_ref, o1_ref, r1_ref, ow_ref, rw_ref, *refs):
        if last:
            out_own, out_ret, dx_ref, att_ref, flag_ref, acc = refs
        else:
            dx_ref, flag_ref, acc = refs
        flag_ref[...] = jnp.zeros_like(flag_ref)
        mine = scal_ref[32]
        total = None
        for part in range(3):
            left = jnp.concatenate([d0_ref[1 + part], d1_ref[1 + part]], axis=1)
            term = over_columns(left, w_ref[:, part * 1024 : part * 1024 + 256])
            total = term if total is None else total + term
        acc[...] = total
        for group, base, own, ret in (
            (1, 0, o1_ref, r1_ref), (2, 0, ow_ref, rw_ref), (3, 256, ow_ref, rw_ref),
        ):
            span = SPANS[group]
            rows = ROWS // span
            low = first_head((rows, BLK))
            zero = jnp.zeros((), BF)
            for src, pair in ((own, mine), (ret, 1 - mine)):
                weights = []
                for part in range(3):
                    col = pl.multiple_of(part * 1024 + group * 256 + pair * BLK, BLK)
                    weights.append(w_ref[:, pl.ds(col, BLK)])
                d_q, d_k, d_v = [src[part, base : base + rows, :] for part in range(3)]
                for head in range(2):
                    if head == 0:
                        d_v_head = jnp.where(low, d_v, zero)
                    else:
                        d_v_head = jnp.where(low, zero, d_v)
                    left = head_columns(d_q, d_k, d_v_head, head)
                    res = over_columns(left, head_columns(*weights, head))
                    off = scal_ref[group * 4 + 2 * pair + head]
                    for r in range(8 // span):
                        at = pl.ds(pl.multiple_of((r * span + off) * BLK, BLK), BLK)
                        acc[at, :] += res[r * BLK : r * BLK + BLK, :]
        dx_ref[...] = acc[...].astype(BF)
        if last:
            low = first_head((BLK, BLK))
            att_ref[:, 0:BLK] = d0_ref[0]
            att_ref[:, BLK : 2 * BLK] = d1_ref[0]
            for group, base in ((1, 0), (2, 512), (3, 768)):
                span = SPANS[group]
                for src, pair in ((out_own, mine), (out_ret, 1 - mine)):
                    off_a = scal_ref[group * 4 + 2 * pair]
                    off_b = scal_ref[group * 4 + 2 * pair + 1]
                    lanes = pl.ds(pl.multiple_of(group * 256 + pair * BLK, BLK), BLK)
                    for block in range(8):
                        mask = block_mask(block, span, off_a, off_b, low)
                        row = base + (block // span) * BLK
                        val = src[row : row + BLK, :]
                        rows = slice(block * BLK, block * BLK + BLK)
                        att_ref[rows, lanes] = jnp.where(mask, val, jnp.zeros((), BF))

    out = jax.ShapeDtypeStruct((ROWS, 1024), BF)
    dx_spec = pl.BlockSpec((ROWS, width), lambda i, s: (0, piece))
    given = () if start else (before,)
    flag_spec = pl.BlockSpec((8, BLK), lambda i, s: (0, 0))
    att_spec = pl.BlockSpec((ROWS, 1024), lambda i, s: (0, 0))
    n_in = 8 + len(outs_of)
    return pl.pallas_call(
        with_order(body, n_in, len(given) + len(deps)),
        grid_spec=pltpu.PrefetchScalarGridSpec(
            num_scalar_prefetch=1,
            grid=(1,),
            in_specs=[pl.BlockSpec((width, 3072), lambda i, s: (piece, 0))]
            + [WHOLE] * (6 + len(outs_of))
            + [ANY] * (len(given) + len(deps)),
            out_specs=[dx_spec] + [att_spec] * last + [flag_spec],
            scratch_shapes=[pltpu.VMEM((ROWS, width), F32)],
        ),
        out_shape=[out] + [out] * last + [jax.ShapeDtypeStruct((8, BLK), F32)],
        input_output_aliases={} if start else {n_in: 0},
        compiler_params=params(),
        cost_estimate=cost(1e6, 1e4),
        name="token_grad",
    )(scal, w_qkv, dense[0], dense[1], one[0], one[1], wide[0], wide[1], *outs_of, *given, *deps)


def fold_add(own, recv, dtype, deps=()):
    def body(own_ref, recv_ref, out_ref):
        out_ref[...] = (own_ref[...].astype(F32) + recv_ref[...].astype(F32)).astype(dtype)

    return pl.pallas_call(
        with_order(body, 2, len(deps)),
        in_specs=[WHOLE] * 2 + [ANY] * len(deps),
        out_shape=jax.ShapeDtypeStruct(own.shape, dtype),
        compiler_params=params(),
        cost_estimate=cost(1e6, 1e4),
        name="fold_add",
    )(own, recv, *deps)


def place_weights(scal, parts, groups_of):
    def body(scal_ref, *refs):
        out = refs[-1]
        core = scal_ref[33]
        at = 0
        for groups in groups_of:
            for pair in (core, 1 - core):
                for n, group in enumerate(groups):
                    for part in range(3):
                        row = n * 192 + part * 64
                        far = len(groups) * 192 + row
                        val = jnp.concatenate(
                            [refs[at][row : row + 64, :], refs[at][far : far + 64, :]], axis=0
                        )
                        col = pl.multiple_of(part * 1024 + group * 256 + pair * BLK, BLK)
                        out[:, pl.ds(col, BLK)] = val.T
                at += 1

    return pl.pallas_call(
        body,
        in_specs=[pl.BlockSpec(memory_space=pltpu.SMEM)] + [WHOLE] * len(parts),
        out_shape=jax.ShapeDtypeStruct((BLK, 3072), F32),
        compiler_params=params(),
        cost_estimate=cost(1e6, 1e4),
        name="place_weights",
    )(scal, *parts)


def per_device(tokens, w_qkv, offsets, d_attended):
    inputs = tokens[0]
    incoming = d_attended[0]
    seq = lax.axis_index("seq")
    core = lax.axis_index("dp") & 1
    b0, b1, b2 = seq & 1, (seq >> 1) & 1, (seq >> 2) & 1
    gray = b1 ^ b2

    def start_p(j, f):
        return 2 * j + (f ^ j)

    def start_q(j, f):
        return 2 * f + j

    tail = [b0, core]
    tail += [start_p(0, 1 - gray), start_p(1, 1 - gray), start_p(0, gray), start_p(1, gray)]
    tail += [start_q(0, 1 - b2), start_q(1, 1 - b2), start_q(0, b2), start_q(1, b2)]
    tail += [b1, b2]
    tail = [jnp.asarray(t, jnp.int32) for t in tail]
    row = offsets[0]
    row_other = swap(row, "dp", 1)
    scal = jnp.concatenate([row, row, jnp.stack(tail)])
    scal_two = jnp.concatenate([row, row_other, jnp.stack(tail)])
    table_p, table_q = 34, 38

    inputs_other = swap(inputs, "dp", 1)

    keep_w, send_w, do_keep, do_send, do_0 = project_groups(inputs, w_qkv, incoming, scal, (2, 3))
    recv_w = swap(send_w, "seq", 1)
    keep_1, send_1 = project_groups(inputs, w_qkv, (do_keep, do_send), scal, (1,), (keep_w,))
    recv_1 = swap(send_1, "seq", 1)
    qkv_0 = project_dense(inputs, w_qkv, (keep_1, inputs_other, scal_two))

    kv_2, kv_3 = pack_pairs(keep_w, recv_w, (qkv_0,))
    from_2 = swap(kv_2, "seq", 2)
    from_4 = swap(kv_3, "seq", 4)
    from_6 = swap(kv_3, "seq", 6)

    dense_0 = attention_dense(qkv_0, do_0, 0, (kv_3,))
    wide = attention_wide(keep_w, recv_w, from_2, from_4, from_6, (dense_0,))
    oq2, loc2, oq3, loc3, to2, to4, to6 = wide
    ret2 = swap(to2, "seq", 2)
    ret4 = swap(to4, "seq", 4)
    ret6 = swap(to6, "seq", 6)
    own_1, back_1, out_one = attention_two(keep_1, recv_1, (oq2,))
    ret_1 = swap(back_1, "seq", 1)
    own_w, back_w, out_own, out_back = combine_wide(
        oq2, loc2, oq3, loc3, ret2, ret4, ret6, out_one, (own_1,)
    )
    ret_w = swap(back_w, "seq", 1)
    dense_1 = attention_dense(qkv_0, do_0, 1, (own_w,))
    dense = (dense_0, dense_1)
    one = (own_1, ret_1)
    far = (own_w, ret_w)

    mine_m, other_m = choose_pairs(scal, (dense, one), 1e6)
    core_m = swap(other_m, "dp", 1)
    mine_f, other_f = choose_pairs(scal, (far,), 10e9, (mine_m,))
    core_f = swap(other_f, "dp", 1)
    grads_m = weight_grad(inputs, inputs_other, scal_two, (0, 1), mine_m, core_m, 10e9, (mine_f,))
    grads_f = weight_grad(inputs, inputs_other, scal_two, (2, 3), mine_f, core_f, 1e6, (grads_m[0],))

    def first_swap(grads):
        send_p, keep_p, send_q, keep_q = grads
        return keep_p, swap(send_p, "seq", 2), keep_q, swap(send_q, "seq", 6)

    def second_swap(folded):
        stay_p, leave_p, stay_q, leave_q = folded
        return stay_p, swap(leave_p, "seq", 6), stay_q, swap(leave_q, "seq", 2)

    def reduce_rest(total, masks):
        half = total
        for mask in masks[:2]:
            total = half.astype(F32) + swap(half, "dp", mask).astype(F32)
            half = total.astype(BF)
        total = total + swap(total, "dp", masks[2])
        return [total, swap(total, "dp", 1)]

    def tokens_part(width, piece, before, dep, outs_of=()):
        return token_grad(w_qkv, scal, dense, one, far, width, piece, before, outs_of, (dep,))

    d_part, flag = tokens_part(512, 0, None, grads_f[0])
    folded_m = fold_x(scal, *first_swap(grads_m), (flag,))
    folded_f = fold_x(scal, *first_swap(grads_f), (folded_m[0],))
    d_part, flag = tokens_part(256, 2, d_part, folded_f[0])
    stay_m, leave_m = fold_y(scal, *second_swap(folded_m), (flag,))
    stay_f, leave_f = fold_y(scal, *second_swap(folded_f), (stay_m,))
    recv_m = swap(leave_m, "seq", 1)
    recv_f = swap(leave_f, "seq", 1)
    out_ret = swap(out_back, "seq", 1)
    d_inputs, attended, flag = tokens_part(256, 3, d_part, stay_f, (out_own, out_ret))
    half_m = fold_add(stay_m, recv_m, BF, (flag,))
    half_f = fold_add(stay_f, recv_f, BF, (half_m,))
    parts = reduce_rest(half_m, (2, 6, 8)) + reduce_rest(half_f, (8, 2, 6))
    d_weights = place_weights(scal, parts, ((0, 1), (2, 3)))
    return (attended[None], d_inputs[None], d_weights)


def solution(mesh):
    placed = (P("dp", "seq", None), P(), P("dp", None), P("dp", "seq", None))
    return jax.shard_map(
        per_device,
        mesh=mesh,
        in_specs=placed,
        out_specs=(P("dp", "seq", None), P("dp", "seq", None), P("seq", None)),
        check_vma=False,
    )
```

```python
import jax
import jax.numpy as jnp
from jax import lax
from jax.experimental import pallas as pl
from jax.experimental.pallas import tpu as pltpu
from jax.sharding import PartitionSpec as P

BLK = 128
ROWS = 1024
BF = jnp.bfloat16
F32 = jnp.float32
SPANS = (1, 2, 4, 8)
VMEM_LIMIT = 48 * 1024 * 1024


def swap(block, axis, mask):
    count = lax.axis_size(axis)
    return lax.ppermute(block, axis, [(i, i ^ mask) for i in range(count)])


def dot(left, right):
    return jnp.dot(left, right, preferred_element_type=F32)


def params(semantics=None):
    return pltpu.CompilerParams(vmem_limit_bytes=VMEM_LIMIT, dimension_semantics=semantics)


def cost(flops, nbytes):
    return pl.CostEstimate(flops=int(flops), bytes_accessed=int(nbytes), transcendentals=0)


def with_order(body, n_in, n_dep):
    def ordered(*refs):
        return body(*refs[:n_in], *refs[n_in + n_dep :])

    return ordered


ANY = pl.BlockSpec(memory_space=pl.ANY)
WHOLE = pl.BlockSpec(memory_space=pltpu.VMEM)


def first_head(shape):
    return lax.broadcasted_iota(jnp.int32, shape, len(shape) - 1) < 64


def turn(block):
    return pltpu.roll(block.astype(F32), 64, axis=1).astype(block.dtype)


def head_columns(query, key, value, head):
    low = first_head(query.shape)
    if head == 0:
        return jnp.concatenate([jnp.where(low, query, turn(key)), value], axis=1)
    return jnp.concatenate([jnp.where(low, turn(query), key), value], axis=1)


def project_groups(tokens, w_qkv, scal, groups, incoming=(), deps=()):
    total = sum(ROWS // SPANS[g] for g in groups)
    wide = len(groups) == 2

    def pick_incoming(in_ref, dst, base, group, pair):
        low = first_head((BLK, BLK))
        span = SPANS[group]
        lanes = pl.ds(pl.multiple_of(group * 256 + pair * BLK, BLK), BLK)
        offs = [scal_of[0][group * 4 + 2 * pair + head] for head in range(2)]
        for r in range(8 // span):
            blks = []
            for head in range(2):
                row = pl.multiple_of((r * span + offs[head]) * BLK, BLK)
                blks.append(in_ref[pl.ds(row, BLK), lanes])
            dst[base + r * BLK : base + r * BLK + BLK, :] = jnp.where(low, blks[0], blks[1])

    scal_of = []

    def body(scal_ref, tok_ref, wq_ref, wk_ref, wv_ref, *refs):
        which = pl.program_id(0)
        mine = scal_ref[32]
        x_s = refs[-1]
        if wide:
            keep_ref, send_ref = refs[:2]
        else:
            in_ref, keep_ref, send_ref, zero_ref = refs[:4]

        def work(group, base):
            span = SPANS[group]
            rows = ROWS // span
            low = first_head((rows, BLK))
            for dst, pair in ((keep_ref, mine), (send_ref, 1 - mine)):
                lanes = pl.ds(pl.multiple_of(pair * BLK, BLK), BLK)
                offs = [scal_ref[group * 4 + 2 * pair + head] for head in range(2)]
                res = []
                for head in range(2):
                    for r in range(8 // span):
                        row = pl.multiple_of((r * span + offs[head]) * BLK, BLK)
                        x_s[r * BLK : r * BLK + BLK, :] = tok_ref[pl.ds(row, BLK), :]
                    cols = head_columns(wq_ref[:, lanes], wk_ref[:, lanes], wv_ref[:, lanes], head)
                    res.append(dot(x_s[:rows, :], cols))
                front = [r[:, :BLK] for r in res]
                back = [r[:, BLK:] for r in res]
                vals = (
                    jnp.where(low, front[0], turn(front[1])),
                    jnp.where(low, turn(front[0]), front[1]),
                    jnp.where(low, back[0], back[1]),
                )
                for slot, val in enumerate(vals):
                    if wide:
                        dst[slot, base : base + rows, :] = val.astype(BF)
                    else:
                        dst[slot * rows : slot * rows + rows, :] = val.astype(BF)

        base = 0
        for n, group in enumerate(groups):

            @pl.when(which == n)
            def _(group=group, base=base):
                work(group, base)

            base += ROWS // SPANS[group]
        if not wide:
            scal_of.append(scal_ref)
            zero_ref[0] = in_ref[:, 0:BLK]
            zero_ref[1] = in_ref[:, BLK : 2 * BLK]
            for dst, pair in ((keep_ref, mine), (send_ref, 1 - mine)):
                for group, at in ((1, 1536), (2, 2048), (3, 2304)):
                    pick_incoming(in_ref, dst, at, group, pair)
            scal_of.clear()

    first = groups[0]
    if wide:
        shapes = [(3, total, BLK)] * 2
    else:
        shapes = [(2432, BLK)] * 2 + [(2, ROWS, BLK)]
    return pl.pallas_call(
        with_order(body, 5 + len(incoming), len(deps)),
        grid_spec=pltpu.PrefetchScalarGridSpec(
            num_scalar_prefetch=1,
            grid=(len(groups),),
            in_specs=[WHOLE]
            + [
                pl.BlockSpec((1024, 256), lambda i, s, part=part: (0, part * 4 + first + i))
                for part in range(3)
            ]
            + [WHOLE] * len(incoming)
            + [ANY] * len(deps),
            out_specs=[
                pl.BlockSpec(shape, lambda i, s, n=len(shape): (0,) * n) for shape in shapes
            ],
            scratch_shapes=[pltpu.VMEM((ROWS // SPANS[first], 1024), BF)],
        ),
        out_shape=[jax.ShapeDtypeStruct(shape, BF) for shape in shapes],
        compiler_params=params(),
        cost_estimate=cost(len(groups) * 2 * 1024 * 1024 * 768, 6e6),
        name="project_kept",
    )(scal, tokens, w_qkv, w_qkv, w_qkv, *incoming, *deps)


def project_dense(tokens, w_qkv, deps=()):
    def body(tok_ref, w_ref, out_ref):
        res = dot(tok_ref[...], w_ref[...]).astype(BF)
        out_ref[0, 0] = res[:, :BLK]
        out_ref[0, 1] = res[:, BLK:]

    return pl.pallas_call(
        with_order(body, 2, len(deps)),
        grid=(3,),
        in_specs=[
            WHOLE,
            pl.BlockSpec((1024, 256), lambda j: (0, j * 4)),
        ]
        + [ANY] * len(deps),
        out_specs=pl.BlockSpec((1, 2, ROWS, BLK), lambda j: (j, 0, 0, 0)),
        out_shape=jax.ShapeDtypeStruct((3, 2, ROWS, BLK), BF),
        compiler_params=params(),
        cost_estimate=cost(2 * 1024 * 1024 * 768, 5e6),
        name="project_dense",
    )(tokens, w_qkv, *deps)


def pair_core(q_s, do_s, k_s, v_s, kt_s, vt_s, o_s, dq_s, dk_s, dv_s, q_rows):
    kt_s[...] = k_s[...].T
    vt_s[...] = v_s[...].T
    low_lane = first_head((q_rows, BLK))
    low_row = lax.broadcasted_iota(jnp.int32, (BLK, q_rows), 0) < 64
    zero = jnp.zeros((), BF)

    q_c = q_s[:q_rows, :] * jnp.asarray(0.125, BF)
    do_c = do_s[:q_rows, :]
    q_t = q_c.T
    do_t = do_c.T
    outs, dqs, probs, d_scores, dos, qs = [], [], [], [], [], []
    for a in range(2):
        mask = low_row if a == 0 else jnp.logical_not(low_row)
        lanes = low_lane if a == 0 else jnp.logical_not(low_lane)
        part = slice(a * 64, a * 64 + 64)
        scores = dot(k_s[...], jnp.where(mask, q_t, zero))
        top = jnp.max(scores, axis=0, keepdims=True)
        e = jnp.exp(scores - top)
        total = jnp.sum(e, axis=0, keepdims=True)
        prob = e * (1.0 / total)
        prob_b = prob.astype(BF)
        out_b = dot(vt_s[part, :], prob_b).astype(BF)
        delta = jnp.sum(do_t[part, :].astype(F32) * out_b.astype(F32), axis=0, keepdims=True)
        d_prob = dot(v_s[...], jnp.where(mask, do_t, zero))
        d_score = (prob * (d_prob - delta)).astype(BF)
        dqs.append(dot(kt_s[part, :], d_score) * 0.125)
        outs.append(out_b)
        probs.append(prob_b)
        d_scores.append(d_score)
        dos.append(jnp.where(lanes, do_c, zero))
        qs.append(jnp.where(lanes, q_c, zero))
    dv_s[...] = dot(jnp.concatenate(probs, axis=1), jnp.concatenate(dos, axis=0))
    dk_s[...] = dot(jnp.concatenate(d_scores, axis=1), jnp.concatenate(qs, axis=0))
    o_s[:q_rows, :] = jnp.concatenate(outs, axis=0).T
    dq_s[:q_rows, :] = jnp.concatenate(dqs, axis=0).T.astype(BF)


def attention_scratch(q_rows):
    return [
        pltpu.VMEM((q_rows, BLK), BF),
        pltpu.VMEM((q_rows, BLK), BF),
        pltpu.VMEM((ROWS, BLK), BF),
        pltpu.VMEM((ROWS, BLK), BF),
        pltpu.VMEM((BLK, ROWS), BF),
        pltpu.VMEM((BLK, ROWS), BF),
        pltpu.VMEM((q_rows, BLK), BF),
        pltpu.VMEM((q_rows, BLK), BF),
        pltpu.VMEM((ROWS, BLK), F32),
        pltpu.VMEM((ROWS, BLK), F32),
    ]


HEAD_FLOPS = 6 * 2 * 1024 * 1024 * 256


def attention_dense(qkv, incoming, pair, deps=()):
    def body(qkv_ref, do_ref, out_ref, kt_s, vt_s, dk_s, dv_s):
        pair_core(
            qkv_ref.at[0, 0], do_ref.at[0], qkv_ref.at[1, 0], qkv_ref.at[2, 0], kt_s, vt_s,
            out_ref.at[0], out_ref.at[1], dk_s, dv_s, ROWS,
        )
        out_ref[2] = dk_s[...].astype(BF)
        out_ref[3] = dv_s[...].astype(BF)

    return pl.pallas_call(
        with_order(body, 2, len(deps)),
        grid=(1,),
        in_specs=[
            pl.BlockSpec((3, 1, ROWS, BLK), lambda i: (0, pair, 0, 0)),
            pl.BlockSpec((1, ROWS, BLK), lambda i: (pair, 0, 0)),
        ]
        + [ANY] * len(deps),
        out_specs=pl.BlockSpec((4, ROWS, BLK), lambda i: (0, 0, 0)),
        out_shape=jax.ShapeDtypeStruct((4, ROWS, BLK), BF),
        scratch_shapes=attention_scratch(ROWS)[4:6] + attention_scratch(ROWS)[8:],
        compiler_params=params(),
        cost_estimate=cost(2 * HEAD_FLOPS, 2e6),
        name="attention_dense",
    )(qkv, incoming, *deps)


def attention_two(keep, recv, deps=()):
    half = ROWS // 2

    def body(keep_ref, recv_ref, own_ref, back_ref, out_ref, *scratch):
        q_s, do_s, k_s, v_s, kt_s, vt_s, o_s, dq_s, dk_s, dv_s = scratch
        for slot, dst in ((0, q_s), (1, k_s), (2, v_s), (3, do_s)):
            rows = slice(slot * half, slot * half + half)
            dst[:half, :] = keep_ref[rows, :]
            dst[half:, :] = recv_ref[rows, :]
        pair_core(q_s, do_s, k_s, v_s, kt_s, vt_s, o_s, dq_s, dk_s, dv_s, ROWS)
        for slot, src in ((0, dq_s), (1, dk_s), (2, dv_s)):
            own_ref[slot] = src[:half, :].astype(BF)
            back_ref[slot] = src[half:, :].astype(BF)
        out_ref[0] = o_s[:half, :]
        out_ref[1] = o_s[half:, :]

    out = jax.ShapeDtypeStruct((3, half, BLK), BF)
    return pl.pallas_call(
        with_order(body, 2, len(deps)),
        in_specs=[WHOLE] * 2 + [ANY] * len(deps),
        out_shape=[out, out, jax.ShapeDtypeStruct((2, half, BLK), BF)],
        scratch_shapes=attention_scratch(ROWS),
        compiler_params=params(),
        cost_estimate=cost(2 * HEAD_FLOPS, 2e6),
        name="attention_two",
    )(keep, recv, *deps)


def pack_pairs(keep, recv, deps=()):
    def body(keep_ref, recv_ref, all_ref, three_ref):
        for n in range(2):
            for at, src in ((0, keep_ref), (1, recv_ref)):
                two = src[1 + n, 0:256, :]
                three = src[1 + n, 256:384, :]
                all_ref[n, at * 256 : at * 256 + 256, :] = two
                all_ref[n, 512 + at * 128 : 640 + at * 128, :] = three
                three_ref[n, at * 128 : at * 128 + 128, :] = three

    return pl.pallas_call(
        with_order(body, 2, len(deps)),
        in_specs=[WHOLE] * 2 + [ANY] * len(deps),
        out_shape=[jax.ShapeDtypeStruct((2, n, BLK), BF) for n in (768, 256)],
        compiler_params=params(),
        cost_estimate=cost(1e6, 1e4),
        name="pack_pairs",
    )(keep, recv, *deps)


def attention_wide(keep, recv, from_2, from_4, from_6, keep_1, recv_1, deps=()):
    def body(
        keep_ref, recv_ref, f2_ref, f4_ref, f6_ref, keep1_ref, recv1_ref,
        oq2_ref, loc2_ref, oq3_ref, loc3_ref, to2_ref, to4_ref, to6_ref, *scratch,
    ):
        q_s, do_s, k_s, v_s, kt_s, vt_s, o_s, dq_s, dk_s, dv_s = scratch
        q_s[0:256, :] = keep_ref[0, 0:256, :]
        q_s[256:512, :] = recv_ref[0, 0:256, :]
        do_s[0:256, :] = keep1_ref[2048:2304, :]
        do_s[256:512, :] = recv1_ref[2048:2304, :]
        for n, dst in ((0, k_s), (1, v_s)):
            dst[0:256, :] = keep_ref[1 + n, 0:256, :]
            dst[256:512, :] = recv_ref[1 + n, 0:256, :]
            dst[512:, :] = f2_ref[n, 0:512, :]
        pair_core(q_s, do_s, k_s, v_s, kt_s, vt_s, o_s, dq_s, dk_s, dv_s, 512)
        oq2_ref[0] = o_s[...]
        oq2_ref[1] = dq_s[...]
        for n, src in ((0, dk_s), (1, dv_s)):
            loc2_ref[n] = src[:512, :]
            to2_ref[n, 0:512, :] = src[512:, :].astype(BF)
        q_s[0:128, :] = keep_ref[0, 256:384, :]
        q_s[128:256, :] = recv_ref[0, 256:384, :]
        do_s[0:128, :] = keep1_ref[2304:2432, :]
        do_s[128:256, :] = recv1_ref[2304:2432, :]
        for n, dst in ((0, k_s), (1, v_s)):
            dst[0:128, :] = keep_ref[1 + n, 256:384, :]
            dst[128:256, :] = recv_ref[1 + n, 256:384, :]
            dst[256:512, :] = f2_ref[n, 512:768, :]
            dst[512:768, :] = f4_ref[n]
            dst[768:, :] = f6_ref[n]
        pair_core(q_s, do_s, k_s, v_s, kt_s, vt_s, o_s, dq_s, dk_s, dv_s, 256)
        oq3_ref[0] = o_s[:256, :]
        oq3_ref[1] = dq_s[:256, :]
        for n, src in ((0, dk_s), (1, dv_s)):
            loc3_ref[n] = src[:256, :]
            to2_ref[n, 512:768, :] = src[256:512, :].astype(BF)
            to4_ref[n] = src[512:768, :].astype(BF)
            to6_ref[n] = src[768:, :].astype(BF)

    shapes = [
        ((2, 512, BLK), BF), ((2, 512, BLK), F32), ((2, 256, BLK), BF), ((2, 256, BLK), F32),
        ((2, 768, BLK), BF), ((2, 256, BLK), BF), ((2, 256, BLK), BF),
    ]
    return pl.pallas_call(
        with_order(body, 7, len(deps)),
        in_specs=[WHOLE] * 7 + [ANY] * len(deps),
        out_shape=[jax.ShapeDtypeStruct(s, d) for s, d in shapes],
        scratch_shapes=attention_scratch(512),
        compiler_params=params(),
        cost_estimate=cost(1.5 * HEAD_FLOPS, 2e6),
        name="attention_wide",
    )(keep, recv, from_2, from_4, from_6, keep_1, recv_1, *deps)


def combine_wide(oq2, loc2, oq3, loc3, ret2, ret4, ret6, out_one, deps=()):
    def body(oq2_ref, loc2_ref, oq3_ref, loc3_ref, r2_ref, r4_ref, r6_ref, one_ref, *refs):
        own_ref, back_ref, out_own, out_back = refs
        for n, (dst, out, at2, at3) in enumerate(
            ((own_ref, out_own, 0, 0), (back_ref, out_back, 256, 128))
        ):
            two = slice(at2, at2 + 256)
            three = slice(at3, at3 + 128)
            out[0:512, :] = one_ref[n]
            out[512:768, :] = oq2_ref[0, two, :]
            out[768:896, :] = oq3_ref[0, three, :]
            dst[0, 0:256, :] = oq2_ref[1, two, :]
            dst[0, 256:384, :] = oq3_ref[1, three, :]
            for n in range(2):
                dst[1 + n, 0:256, :] = (loc2_ref[n, two, :] + r2_ref[n, two, :].astype(F32)).astype(BF)
                far = r4_ref[n, three, :].astype(F32) + r6_ref[n, three, :].astype(F32)
                near = r2_ref[n, 512 + at3 : 640 + at3, :].astype(F32)
                dst[1 + n, 256:384, :] = (loc3_ref[n, three, :] + near + far).astype(BF)

    shapes = [(3, 384, BLK)] * 2 + [(896, BLK)] * 2
    return pl.pallas_call(
        with_order(body, 8, len(deps)),
        in_specs=[WHOLE] * 8 + [ANY] * len(deps),
        out_shape=[jax.ShapeDtypeStruct(shape, BF) for shape in shapes],
        compiler_params=params(),
        cost_estimate=cost(1e6, 1e4),
        name="combine_wide",
    )(oq2, loc2, oq3, loc3, ret2, ret4, ret6, out_one, *deps)


def choose_pairs(scal, sources, weight, deps=()):
    slabs = [src[0].shape[1] for src in sources]
    total = sum(slabs)

    def body(scal_ref, *refs):
        mine_ref, other_ref = refs[-2:]
        core = scal_ref[33]
        base = 0
        for n, slab in enumerate(slabs):
            first, second = refs[2 * n : 2 * n + 2]
            same = core == (0 if slab == ROWS else scal_ref[32])
            here = slice(base, base + slab)

            def copy(one, two, here=here, slot=1 if slab == ROWS else 0):
                for part in range(3):
                    mine_ref[part, here, :] = one[slot + part]
                    other_ref[part, here, :] = two[slot + part]

            pl.when(same)(lambda first=first, second=second, copy=copy: copy(first, second))
            pl.when(jnp.logical_not(same))(
                lambda first=first, second=second, copy=copy: copy(second, first)
            )
            base += slab

    flat = [x for source in sources for x in source]
    out = jax.ShapeDtypeStruct((3, total, BLK), BF)
    return pl.pallas_call(
        with_order(body, 1 + len(flat), len(deps)),
        in_specs=[pl.BlockSpec(memory_space=pltpu.SMEM)] + [WHOLE] * len(flat) + [ANY] * len(deps),
        out_shape=[out, out],
        compiler_params=params(),
        cost_estimate=cost(weight, 1e4),
        name="choose_pairs",
    )(scal, *flat, *deps)


def block_mask(block, span, off_a, off_b, low):
    here = block % span
    keep_a = jnp.where(off_a == here, 1, 0)
    keep_b = jnp.where(off_b == here, 1, 0)
    return jnp.where(low, keep_a, keep_b) == 1


def weight_grad(tokens, tokens_other, scal, groups, mine, other, weight, deps=()):
    count = len(groups) * 192
    tables = (34, 38)

    def body(scal_ref, tok_ref, tok2_ref, mine_ref, other_ref, *refs):
        outs = refs[:4]
        l_s, x_s = refs[4:]
        core = scal_ref[33]
        base = 0
        for at, group in enumerate(groups):
            span = SPANS[group]
            rows = ROWS // span
            for n, src in ((0, mine_ref), (1, other_ref)):
                to = slice(n * rows, n * rows + rows)
                for part in range(3):
                    val = src[part, base : base + rows, :].T
                    l_s[part * 64 : part * 64 + 64, to] = val[:64]
                    l_s[192 + part * 64 : 256 + part * 64, to] = val[64:]
            base += rows
            for head in range(2):
                left = l_s.at[head * 192 : head * 192 + 192, :]
                starts = [pl.multiple_of(scal_ref[tables[head] + j] * 256, 256) for j in range(4)]
                if span > 1:
                    for n, tok in ((0, tok_ref), (1, tok2_ref)):
                        off = scal_ref[n * 16 + group * 4 + 2 * core + head]
                        for r in range(8 // span):
                            row = pl.multiple_of((r * span + off) * BLK, BLK)
                            to = n * rows + r * BLK
                            for j in range(4):
                                x_s[to : to + BLK, j * 256 : j * 256 + 256] = tok[
                                    pl.ds(row, BLK), pl.ds(starts[j], 256)
                                ]
                for j in range(4):
                    if span > 1:
                        res = dot(left[:, : 2 * rows], x_s[: 2 * rows, j * 256 : j * 256 + 256])
                    else:
                        lanes = pl.ds(starts[j], 256)
                        res = dot(left[:, :ROWS], tok_ref[:, lanes])
                        res += dot(left[:, ROWS:], tok2_ref[:, lanes])
                    to = slice(at * 192, at * 192 + 192)
                    if j < 2:
                        outs[2 * head][j, to, :] = res.astype(BF)
                    else:
                        outs[2 * head + 1][j - 2, to, :] = res

    smem = pl.BlockSpec(memory_space=pltpu.SMEM)
    return pl.pallas_call(
        with_order(body, 5, len(deps)),
        in_specs=[smem] + [WHOLE] * 4 + [ANY] * len(deps),
        out_shape=[jax.ShapeDtypeStruct((2, count, 256), d) for d in (BF, F32, BF, F32)],
        scratch_shapes=[
            pltpu.VMEM((384, 2 * ROWS), BF),
            pltpu.VMEM((ROWS, 1024), BF),
        ],
        compiler_params=params(),
        cost_estimate=cost(weight, 1e4),
        name="weight_grad",
    )(scal, tokens, tokens_other, mine, other, *deps)


def fold_x(scal, keep_p, recv_p, keep_q, recv_q, deps=()):
    rows = keep_p.shape[1]

    def body(scal_ref, kp, rp, kq, rq, stay_p, leave_p, stay_q, leave_q):
        for bit, keep, recv, stay, leave in (
            (scal_ref[43], kp, rp, stay_p, leave_p),
            (scal_ref[42], kq, rq, stay_q, leave_q),
        ):
            stay[...] = keep[bit] + recv[bit].astype(F32)
            leave[...] = (keep[1 - bit] + recv[1 - bit].astype(F32)).astype(BF)

    return pl.pallas_call(
        with_order(body, 5, len(deps)),
        in_specs=[pl.BlockSpec(memory_space=pltpu.SMEM)] + [WHOLE] * 4 + [ANY] * len(deps),
        out_shape=[jax.ShapeDtypeStruct((rows, 256), d) for d in (F32, BF, F32, BF)],
        compiler_params=params(),
        cost_estimate=cost(1e6, 1e4),
        name="fold_x",
    )(scal, keep_p, recv_p, keep_q, recv_q, *deps)


def fold_y(scal, stay_p, recv_p, stay_q, recv_q, deps=()):
    rows = stay_p.shape[0]

    def body(scal_ref, sp, rp, sq, rq, stay, leave):
        bit = scal_ref[32]
        here = pl.ds(pl.multiple_of(bit * BLK, BLK), BLK)
        there = pl.ds(pl.multiple_of((1 - bit) * BLK, BLK), BLK)
        for at, own, recv in ((0, sp, rp), (rows, sq, rq)):
            stay[at : at + rows, :] = own[:, here] + recv[:, here].astype(F32)
            leave[at : at + rows, :] = (own[:, there] + recv[:, there].astype(F32)).astype(BF)

    return pl.pallas_call(
        with_order(body, 5, len(deps)),
        in_specs=[pl.BlockSpec(memory_space=pltpu.SMEM)] + [WHOLE] * 4 + [ANY] * len(deps),
        out_shape=[jax.ShapeDtypeStruct((2 * rows, BLK), d) for d in (F32, BF)],
        compiler_params=params(),
        cost_estimate=cost(1e6, 1e4),
        name="fold_y",
    )(scal, stay_p, recv_p, stay_q, recv_q, *deps)


def over_columns(left, right):
    return lax.dot_general(left, right, (((1,), (1,)), ((), ())), preferred_element_type=F32)


def token_grad(w_qkv, scal, dense, one, wide, width, piece, before=None, outs_of=(), deps=()):
    start = before is None
    last = len(outs_of) > 0

    def body(scal_ref, w_ref, d0_ref, d1_ref, o1_ref, r1_ref, ow_ref, rw_ref, *refs):
        if last:
            out_own, out_ret, dx_ref, att_ref, flag_ref, acc = refs
        else:
            dx_ref, flag_ref, acc = refs
        flag_ref[...] = jnp.zeros_like(flag_ref)
        mine = scal_ref[32]
        total = None
        for part in range(3):
            left = jnp.concatenate([d0_ref[1 + part], d1_ref[1 + part]], axis=1)
            term = over_columns(left, w_ref[:, part * 1024 : part * 1024 + 256])
            total = term if total is None else total + term
        acc[...] = total
        for group, base, own, ret in (
            (1, 0, o1_ref, r1_ref), (2, 0, ow_ref, rw_ref), (3, 256, ow_ref, rw_ref),
        ):
            span = SPANS[group]
            rows = ROWS // span
            low = first_head((rows, BLK))
            zero = jnp.zeros((), BF)
            for src, pair in ((own, mine), (ret, 1 - mine)):
                weights = []
                for part in range(3):
                    col = pl.multiple_of(part * 1024 + group * 256 + pair * BLK, BLK)
                    weights.append(w_ref[:, pl.ds(col, BLK)])
                d_q, d_k, d_v = [src[part, base : base + rows, :] for part in range(3)]
                for head in range(2):
                    if head == 0:
                        d_v_head = jnp.where(low, d_v, zero)
                    else:
                        d_v_head = jnp.where(low, zero, d_v)
                    left = head_columns(d_q, d_k, d_v_head, head)
                    res = over_columns(left, head_columns(*weights, head))
                    off = scal_ref[group * 4 + 2 * pair + head]
                    for r in range(8 // span):
                        at = pl.ds(pl.multiple_of((r * span + off) * BLK, BLK), BLK)
                        acc[at, :] += res[r * BLK : r * BLK + BLK, :]
        dx_ref[...] = acc[...].astype(BF)
        if last:
            low = first_head((BLK, BLK))
            att_ref[:, 0:BLK] = d0_ref[0]
            att_ref[:, BLK : 2 * BLK] = d1_ref[0]
            for group, base in ((1, 0), (2, 512), (3, 768)):
                span = SPANS[group]
                for src, pair in ((out_own, mine), (out_ret, 1 - mine)):
                    off_a = scal_ref[group * 4 + 2 * pair]
                    off_b = scal_ref[group * 4 + 2 * pair + 1]
                    lanes = pl.ds(pl.multiple_of(group * 256 + pair * BLK, BLK), BLK)
                    for block in range(8):
                        mask = block_mask(block, span, off_a, off_b, low)
                        row = base + (block // span) * BLK
                        val = src[row : row + BLK, :]
                        rows = slice(block * BLK, block * BLK + BLK)
                        att_ref[rows, lanes] = jnp.where(mask, val, jnp.zeros((), BF))

    out = jax.ShapeDtypeStruct((ROWS, 1024), BF)
    dx_spec = pl.BlockSpec((ROWS, width), lambda i, s: (0, piece))
    given = () if start else (before,)
    flag_spec = pl.BlockSpec((8, BLK), lambda i, s: (0, 0))
    att_spec = pl.BlockSpec((ROWS, 1024), lambda i, s: (0, 0))
    n_in = 8 + len(outs_of)
    return pl.pallas_call(
        with_order(body, n_in, len(given) + len(deps)),
        grid_spec=pltpu.PrefetchScalarGridSpec(
            num_scalar_prefetch=1,
            grid=(1,),
            in_specs=[pl.BlockSpec((width, 3072), lambda i, s: (piece, 0))]
            + [WHOLE] * (6 + len(outs_of))
            + [ANY] * (len(given) + len(deps)),
            out_specs=[dx_spec] + [att_spec] * last + [flag_spec],
            scratch_shapes=[pltpu.VMEM((ROWS, width), F32)],
        ),
        out_shape=[out] + [out] * last + [jax.ShapeDtypeStruct((8, BLK), F32)],
        input_output_aliases={} if start else {n_in: 0},
        compiler_params=params(),
        cost_estimate=cost(1e6, 1e4),
        name="token_grad",
    )(scal, w_qkv, dense[0], dense[1], one[0], one[1], wide[0], wide[1], *outs_of, *given, *deps)


def fold_add(own, recv, dtype, deps=()):
    def body(own_ref, recv_ref, out_ref):
        out_ref[...] = (own_ref[...].astype(F32) + recv_ref[...].astype(F32)).astype(dtype)

    return pl.pallas_call(
        with_order(body, 2, len(deps)),
        in_specs=[WHOLE] * 2 + [ANY] * len(deps),
        out_shape=jax.ShapeDtypeStruct(own.shape, dtype),
        compiler_params=params(),
        cost_estimate=cost(1e6, 1e4),
        name="fold_add",
    )(own, recv, *deps)


def place_weights(scal, parts, groups_of):
    def body(scal_ref, *refs):
        out = refs[-1]
        core = scal_ref[33]
        at = 0
        for groups in groups_of:
            for pair in (core, 1 - core):
                for n, group in enumerate(groups):
                    for part in range(3):
                        row = n * 192 + part * 64
                        far = len(groups) * 192 + row
                        val = jnp.concatenate(
                            [refs[at][row : row + 64, :], refs[at][far : far + 64, :]], axis=0
                        )
                        col = pl.multiple_of(part * 1024 + group * 256 + pair * BLK, BLK)
                        out[:, pl.ds(col, BLK)] = val.T
                at += 1

    return pl.pallas_call(
        body,
        in_specs=[pl.BlockSpec(memory_space=pltpu.SMEM)] + [WHOLE] * len(parts),
        out_shape=jax.ShapeDtypeStruct((BLK, 3072), F32),
        compiler_params=params(),
        cost_estimate=cost(1e6, 1e4),
        name="place_weights",
    )(scal, *parts)


def per_device(tokens, w_qkv, offsets, d_attended):
    inputs = tokens[0]
    incoming = d_attended[0]
    seq = lax.axis_index("seq")
    core = lax.axis_index("dp") & 1
    b0, b1, b2 = seq & 1, (seq >> 1) & 1, (seq >> 2) & 1
    gray = b1 ^ b2

    def start_p(j, f):
        return 2 * j + (f ^ j)

    def start_q(j, f):
        return 2 * f + j

    tail = [b0, core]
    tail += [start_p(0, 1 - gray), start_p(1, 1 - gray), start_p(0, gray), start_p(1, gray)]
    tail += [start_q(0, 1 - b2), start_q(1, 1 - b2), start_q(0, b2), start_q(1, b2)]
    tail += [b1, b2]
    tail = [jnp.asarray(t, jnp.int32) for t in tail]
    row = offsets[0]
    row_other = swap(row, "dp", 1)
    scal = jnp.concatenate([row, row, jnp.stack(tail)])
    scal_two = jnp.concatenate([row, row_other, jnp.stack(tail)])
    table_p, table_q = 34, 38

    inputs_other = swap(inputs, "dp", 1)

    keep_w, send_w = project_groups(inputs, w_qkv, scal, (2, 3))
    recv_w = swap(send_w, "seq", 1)
    keep_1, send_1, do_0 = project_groups(inputs, w_qkv, scal, (1,), (incoming,), (keep_w,))
    recv_1 = swap(send_1, "seq", 1)
    qkv_0 = project_dense(inputs, w_qkv, (keep_1, inputs_other, scal_two))

    kv_2, kv_3 = pack_pairs(keep_w, recv_w, (qkv_0,))
    from_2 = swap(kv_2, "seq", 2)
    from_4 = swap(kv_3, "seq", 4)
    from_6 = swap(kv_3, "seq", 6)

    dense_0 = attention_dense(qkv_0, do_0, 0, (kv_3,))
    wide = attention_wide(
        keep_w, recv_w, from_2, from_4, from_6, keep_1, recv_1, (dense_0,)
    )
    oq2, loc2, oq3, loc3, to2, to4, to6 = wide
    ret2 = swap(to2, "seq", 2)
    ret4 = swap(to4, "seq", 4)
    ret6 = swap(to6, "seq", 6)
    own_1, back_1, out_one = attention_two(keep_1, recv_1, (oq2,))
    ret_1 = swap(back_1, "seq", 1)
    own_w, back_w, out_own, out_back = combine_wide(
        oq2, loc2, oq3, loc3, ret2, ret4, ret6, out_one, (own_1,)
    )
    ret_w = swap(back_w, "seq", 1)
    dense_1 = attention_dense(qkv_0, do_0, 1, (own_w,))
    dense = (dense_0, dense_1)
    one = (own_1, ret_1)
    far = (own_w, ret_w)

    mine_m, other_m = choose_pairs(scal, (dense, one), 1e6)
    core_m = swap(other_m, "dp", 1)
    mine_f, other_f = choose_pairs(scal, (far,), 10e9, (mine_m,))
    core_f = swap(other_f, "dp", 1)
    grads_m = weight_grad(inputs, inputs_other, scal_two, (0, 1), mine_m, core_m, 10e9, (mine_f,))
    grads_f = weight_grad(inputs, inputs_other, scal_two, (2, 3), mine_f, core_f, 1e6, (grads_m[0],))

    def first_swap(grads):
        send_p, keep_p, send_q, keep_q = grads
        return keep_p, swap(send_p, "seq", 2), keep_q, swap(send_q, "seq", 6)

    def second_swap(folded):
        stay_p, leave_p, stay_q, leave_q = folded
        return stay_p, swap(leave_p, "seq", 6), stay_q, swap(leave_q, "seq", 2)

    def reduce_rest(total, masks):
        half = total
        for mask in masks[:2]:
            total = half.astype(F32) + swap(half, "dp", mask).astype(F32)
            half = total.astype(BF)
        total = total + swap(total, "dp", masks[2])
        return [total, swap(total, "dp", 1)]

    def tokens_part(width, piece, before, dep, outs_of=()):
        return token_grad(w_qkv, scal, dense, one, far, width, piece, before, outs_of, (dep,))

    d_part, flag = tokens_part(512, 0, None, grads_f[0])
    folded_m = fold_x(scal, *first_swap(grads_m), (flag,))
    folded_f = fold_x(scal, *first_swap(grads_f), (folded_m[0],))
    d_part, flag = tokens_part(256, 2, d_part, folded_f[0])
    stay_m, leave_m = fold_y(scal, *second_swap(folded_m), (flag,))
    stay_f, leave_f = fold_y(scal, *second_swap(folded_f), (stay_m,))
    recv_m = swap(leave_m, "seq", 1)
    recv_f = swap(leave_f, "seq", 1)
    out_ret = swap(out_back, "seq", 1)
    d_inputs, attended, flag = tokens_part(256, 3, d_part, stay_f, (out_own, out_ret))
    half_m = fold_add(stay_m, recv_m, BF, (flag,))
    half_f = fold_add(stay_f, recv_f, BF, (half_m,))
    parts = reduce_rest(half_m, (2, 6, 8)) + reduce_rest(half_f, (8, 2, 6))
    d_weights = place_weights(scal, parts, ((0, 1), (2, 3)))
    return (attended[None], d_inputs[None], d_weights)


def solution(mesh):
    placed = (P("dp", "seq", None), P(), P("dp", None), P("dp", "seq", None))
    return jax.shard_map(
        per_device,
        mesh=mesh,
        in_specs=placed,
        out_specs=(P("dp", "seq", None), P("dp", "seq", None), P("seq", None)),
        check_vma=False,
    )
```

```python
import jax
import jax.numpy as jnp
from jax import lax
from jax.experimental import pallas as pl
from jax.experimental.pallas import tpu as pltpu
from jax.sharding import PartitionSpec as P

BLK = 128
ROWS = 1024
BF = jnp.bfloat16
F32 = jnp.float32
SPANS = (1, 2, 4, 8)
VMEM_LIMIT = 48 * 1024 * 1024


def swap(block, axis, mask):
    count = lax.axis_size(axis)
    return lax.ppermute(block, axis, [(i, i ^ mask) for i in range(count)])


def dot(left, right):
    return jnp.dot(left, right, preferred_element_type=F32)


def params(semantics=None):
    return pltpu.CompilerParams(vmem_limit_bytes=VMEM_LIMIT, dimension_semantics=semantics)


def cost(flops, nbytes):
    return pl.CostEstimate(flops=int(flops), bytes_accessed=int(nbytes), transcendentals=0)


def with_order(body, n_in, n_dep):
    def ordered(*refs):
        return body(*refs[:n_in], *refs[n_in + n_dep :])

    return ordered


ANY = pl.BlockSpec(memory_space=pl.ANY)
WHOLE = pl.BlockSpec(memory_space=pltpu.VMEM)


def first_head(shape):
    return lax.broadcasted_iota(jnp.int32, shape, len(shape) - 1) < 64


def turn(block):
    return pltpu.roll(block.astype(F32), 64, axis=1).astype(block.dtype)


def head_columns(query, key, value, head):
    low = first_head(query.shape)
    if head == 0:
        return jnp.concatenate([jnp.where(low, query, turn(key)), value], axis=1)
    return jnp.concatenate([jnp.where(low, turn(query), key), value], axis=1)


def project_groups(tokens, w_qkv, scal, groups, incoming=(), deps=()):
    total = sum(ROWS // SPANS[g] for g in groups)
    wide = len(groups) == 2

    def pick_incoming(in_ref, dst, base, group, pair):
        low = first_head((BLK, BLK))
        span = SPANS[group]
        lanes = pl.ds(pl.multiple_of(group * 256 + pair * BLK, BLK), BLK)
        offs = [scal_of[0][group * 4 + 2 * pair + head] for head in range(2)]
        for r in range(8 // span):
            blks = []
            for head in range(2):
                row = pl.multiple_of((r * span + offs[head]) * BLK, BLK)
                blks.append(in_ref[pl.ds(row, BLK), lanes])
            dst[base + r * BLK : base + r * BLK + BLK, :] = jnp.where(low, blks[0], blks[1])

    scal_of = []

    def body(scal_ref, tok_ref, wq_ref, wk_ref, wv_ref, *refs):
        which = pl.program_id(0)
        mine = scal_ref[32]
        x_s = refs[-1]
        if wide:
            keep_ref, send_ref = refs[:2]
        else:
            in_ref, keep_ref, send_ref, zero_ref = refs[:4]

        def work(group, base):
            span = SPANS[group]
            rows = ROWS // span
            low = first_head((rows, BLK))
            for dst, pair in ((keep_ref, mine), (send_ref, 1 - mine)):
                lanes = pl.ds(pl.multiple_of(pair * BLK, BLK), BLK)
                offs = [scal_ref[group * 4 + 2 * pair + head] for head in range(2)]
                res = []
                for head in range(2):
                    for r in range(8 // span):
                        row = pl.multiple_of((r * span + offs[head]) * BLK, BLK)
                        x_s[r * BLK : r * BLK + BLK, :] = tok_ref[pl.ds(row, BLK), :]
                    cols = head_columns(wq_ref[:, lanes], wk_ref[:, lanes], wv_ref[:, lanes], head)
                    res.append(dot(x_s[:rows, :], cols))
                front = [r[:, :BLK] for r in res]
                back = [r[:, BLK:] for r in res]
                vals = (
                    jnp.where(low, front[0], turn(front[1])),
                    jnp.where(low, turn(front[0]), front[1]),
                    jnp.where(low, back[0], back[1]),
                )
                for slot, val in enumerate(vals):
                    if wide:
                        dst[slot, base : base + rows, :] = val.astype(BF)
                    else:
                        dst[slot * rows : slot * rows + rows, :] = val.astype(BF)

        base = 0
        for n, group in enumerate(groups):

            @pl.when(which == n)
            def _(group=group, base=base):
                work(group, base)

            base += ROWS // SPANS[group]
        if not wide:
            scal_of.append(scal_ref)
            zero_ref[0] = in_ref[:, 0:BLK]
            zero_ref[1] = in_ref[:, BLK : 2 * BLK]
            for dst, pair in ((keep_ref, mine), (send_ref, 1 - mine)):
                for group, at in ((1, 1536), (2, 2048), (3, 2304)):
                    pick_incoming(in_ref, dst, at, group, pair)
            scal_of.clear()

    first = groups[0]
    if wide:
        shapes = [(3, total, BLK)] * 2
    else:
        shapes = [(2432, BLK)] * 2 + [(2, ROWS, BLK)]
    return pl.pallas_call(
        with_order(body, 5 + len(incoming), len(deps)),
        grid_spec=pltpu.PrefetchScalarGridSpec(
            num_scalar_prefetch=1,
            grid=(len(groups),),
            in_specs=[WHOLE]
            + [
                pl.BlockSpec((1024, 256), lambda i, s, part=part: (0, part * 4 + first + i))
                for part in range(3)
            ]
            + [WHOLE] * len(incoming)
            + [ANY] * len(deps),
            out_specs=[
                pl.BlockSpec(shape, lambda i, s, n=len(shape): (0,) * n) for shape in shapes
            ],
            scratch_shapes=[pltpu.VMEM((ROWS // SPANS[first], 1024), BF)],
        ),
        out_shape=[jax.ShapeDtypeStruct(shape, BF) for shape in shapes],
        compiler_params=params(),
        cost_estimate=cost(len(groups) * 2 * 1024 * 1024 * 768, 6e6),
        name="project_kept",
    )(scal, tokens, w_qkv, w_qkv, w_qkv, *incoming, *deps)


def project_dense(tokens, w_qkv, deps=()):
    def body(tok_ref, w_ref, out_ref):
        res = dot(tok_ref[...], w_ref[...]).astype(BF)
        out_ref[0, 0] = res[:, :BLK]
        out_ref[0, 1] = res[:, BLK:]

    return pl.pallas_call(
        with_order(body, 2, len(deps)),
        grid=(3,),
        in_specs=[
            WHOLE,
            pl.BlockSpec((1024, 256), lambda j: (0, j * 4)),
        ]
        + [ANY] * len(deps),
        out_specs=pl.BlockSpec((1, 2, ROWS, BLK), lambda j: (j, 0, 0, 0)),
        out_shape=jax.ShapeDtypeStruct((3, 2, ROWS, BLK), BF),
        compiler_params=params(),
        cost_estimate=cost(2 * 1024 * 1024 * 768, 5e6),
        name="project_dense",
    )(tokens, w_qkv, *deps)


def pair_core(q_s, do_s, k_s, v_s, kt_s, vt_s, o_s, dq_s, dk_s, dv_s, q_rows):
    kt_s[...] = k_s[...].T
    vt_s[...] = v_s[...].T
    low_lane = first_head((q_rows, BLK))
    low_row = lax.broadcasted_iota(jnp.int32, (BLK, q_rows), 0) < 64
    zero = jnp.zeros((), BF)

    q_c = q_s[:q_rows, :] * jnp.asarray(0.125, BF)
    do_c = do_s[:q_rows, :]
    q_t = q_c.T
    do_t = do_c.T
    outs, dqs, probs, d_scores, dos, qs = [], [], [], [], [], []
    for a in range(2):
        mask = low_row if a == 0 else jnp.logical_not(low_row)
        lanes = low_lane if a == 0 else jnp.logical_not(low_lane)
        part = slice(a * 64, a * 64 + 64)
        scores = dot(k_s[...], jnp.where(mask, q_t, zero))
        top = jnp.max(scores, axis=0, keepdims=True)
        e = jnp.exp(scores - top)
        total = jnp.sum(e, axis=0, keepdims=True)
        prob = e * (1.0 / total)
        prob_b = prob.astype(BF)
        out_b = dot(vt_s[part, :], prob_b).astype(BF)
        delta = jnp.sum(do_t[part, :].astype(F32) * out_b.astype(F32), axis=0, keepdims=True)
        d_prob = dot(v_s[...], jnp.where(mask, do_t, zero))
        d_score = (prob * (d_prob - delta)).astype(BF)
        dqs.append(dot(kt_s[part, :], d_score) * 0.125)
        outs.append(out_b)
        probs.append(prob_b)
        d_scores.append(d_score)
        dos.append(jnp.where(lanes, do_c, zero))
        qs.append(jnp.where(lanes, q_c, zero))
    dv_s[...] = dot(jnp.concatenate(probs, axis=1), jnp.concatenate(dos, axis=0))
    dk_s[...] = dot(jnp.concatenate(d_scores, axis=1), jnp.concatenate(qs, axis=0))
    o_s[:q_rows, :] = jnp.concatenate(outs, axis=0).T
    dq_s[:q_rows, :] = jnp.concatenate(dqs, axis=0).T.astype(BF)


def attention_scratch(q_rows):
    return [
        pltpu.VMEM((q_rows, BLK), BF),
        pltpu.VMEM((q_rows, BLK), BF),
        pltpu.VMEM((ROWS, BLK), BF),
        pltpu.VMEM((ROWS, BLK), BF),
        pltpu.VMEM((BLK, ROWS), BF),
        pltpu.VMEM((BLK, ROWS), BF),
        pltpu.VMEM((q_rows, BLK), BF),
        pltpu.VMEM((q_rows, BLK), BF),
        pltpu.VMEM((ROWS, BLK), F32),
        pltpu.VMEM((ROWS, BLK), F32),
    ]


HEAD_FLOPS = 6 * 2 * 1024 * 1024 * 256


def attention_dense(qkv, incoming, pair, deps=()):
    def body(qkv_ref, do_ref, out_ref, kt_s, vt_s, dk_s, dv_s):
        pair_core(
            qkv_ref.at[0, 0], do_ref.at[0], qkv_ref.at[1, 0], qkv_ref.at[2, 0], kt_s, vt_s,
            out_ref.at[0], out_ref.at[1], dk_s, dv_s, ROWS,
        )
        out_ref[2] = dk_s[...].astype(BF)
        out_ref[3] = dv_s[...].astype(BF)

    return pl.pallas_call(
        with_order(body, 2, len(deps)),
        grid=(1,),
        in_specs=[
            pl.BlockSpec((3, 1, ROWS, BLK), lambda i: (0, pair, 0, 0)),
            pl.BlockSpec((1, ROWS, BLK), lambda i: (pair, 0, 0)),
        ]
        + [ANY] * len(deps),
        out_specs=pl.BlockSpec((4, ROWS, BLK), lambda i: (0, 0, 0)),
        out_shape=jax.ShapeDtypeStruct((4, ROWS, BLK), BF),
        scratch_shapes=attention_scratch(ROWS)[4:6] + attention_scratch(ROWS)[8:],
        compiler_params=params(),
        cost_estimate=cost(2 * HEAD_FLOPS, 2e6),
        name="attention_dense",
    )(qkv, incoming, *deps)


def attention_two(keep, recv, deps=()):
    half = ROWS // 2

    def body(keep_ref, recv_ref, own_ref, back_ref, out_ref, *scratch):
        q_s, do_s, k_s, v_s, kt_s, vt_s, o_s, dq_s, dk_s, dv_s = scratch
        for slot, dst in ((0, q_s), (1, k_s), (2, v_s), (3, do_s)):
            rows = slice(slot * half, slot * half + half)
            dst[:half, :] = keep_ref[rows, :]
            dst[half:, :] = recv_ref[rows, :]
        pair_core(q_s, do_s, k_s, v_s, kt_s, vt_s, o_s, dq_s, dk_s, dv_s, ROWS)
        for slot, src in ((0, dq_s), (1, dk_s), (2, dv_s)):
            own_ref[slot] = src[:half, :].astype(BF)
            back_ref[slot] = src[half:, :].astype(BF)
        out_ref[0] = o_s[:half, :]
        out_ref[1] = o_s[half:, :]

    out = jax.ShapeDtypeStruct((3, half, BLK), BF)
    return pl.pallas_call(
        with_order(body, 2, len(deps)),
        in_specs=[WHOLE] * 2 + [ANY] * len(deps),
        out_shape=[out, out, jax.ShapeDtypeStruct((2, half, BLK), BF)],
        scratch_shapes=attention_scratch(ROWS),
        compiler_params=params(),
        cost_estimate=cost(2 * HEAD_FLOPS, 2e6),
        name="attention_two",
    )(keep, recv, *deps)


def pack_pairs(keep, recv, deps=()):
    def body(keep_ref, recv_ref, all_ref, three_ref):
        for n in range(2):
            for at, src in ((0, keep_ref), (1, recv_ref)):
                two = src[1 + n, 0:256, :]
                three = src[1 + n, 256:384, :]
                all_ref[n, at * 256 : at * 256 + 256, :] = two
                all_ref[n, 512 + at * 128 : 640 + at * 128, :] = three
                three_ref[n, at * 128 : at * 128 + 128, :] = three

    return pl.pallas_call(
        with_order(body, 2, len(deps)),
        in_specs=[WHOLE] * 2 + [ANY] * len(deps),
        out_shape=[jax.ShapeDtypeStruct((2, n, BLK), BF) for n in (768, 256)],
        compiler_params=params(),
        cost_estimate=cost(1e6, 1e4),
        name="pack_pairs",
    )(keep, recv, *deps)


def attention_wide(keep, recv, from_2, from_4, from_6, keep_1, recv_1, deps=()):
    def body(
        keep_ref, recv_ref, f2_ref, f4_ref, f6_ref, keep1_ref, recv1_ref,
        oq2_ref, loc2_ref, oq3_ref, loc3_ref, to2_ref, to4_ref, to6_ref, *scratch,
    ):
        q_s, do_s, k_s, v_s, kt_s, vt_s, o_s, dq_s, dk_s, dv_s = scratch
        q_s[0:256, :] = keep_ref[0, 0:256, :]
        q_s[256:512, :] = recv_ref[0, 0:256, :]
        do_s[0:256, :] = keep1_ref[2048:2304, :]
        do_s[256:512, :] = recv1_ref[2048:2304, :]
        for n, dst in ((0, k_s), (1, v_s)):
            dst[0:256, :] = keep_ref[1 + n, 0:256, :]
            dst[256:512, :] = recv_ref[1 + n, 0:256, :]
            dst[512:, :] = f2_ref[n, 0:512, :]
        pair_core(q_s, do_s, k_s, v_s, kt_s, vt_s, o_s, dq_s, dk_s, dv_s, 512)
        oq2_ref[0] = o_s[...]
        oq2_ref[1] = dq_s[...]
        for n, src in ((0, dk_s), (1, dv_s)):
            loc2_ref[n] = src[:512, :]
            to2_ref[n, 0:512, :] = src[512:, :].astype(BF)
        q_s[0:128, :] = keep_ref[0, 256:384, :]
        q_s[128:256, :] = recv_ref[0, 256:384, :]
        do_s[0:128, :] = keep1_ref[2304:2432, :]
        do_s[128:256, :] = recv1_ref[2304:2432, :]
        for n, dst in ((0, k_s), (1, v_s)):
            dst[0:128, :] = keep_ref[1 + n, 256:384, :]
            dst[128:256, :] = recv_ref[1 + n, 256:384, :]
            dst[256:512, :] = f2_ref[n, 512:768, :]
            dst[512:768, :] = f4_ref[n]
            dst[768:, :] = f6_ref[n]
        pair_core(q_s, do_s, k_s, v_s, kt_s, vt_s, o_s, dq_s, dk_s, dv_s, 256)
        oq3_ref[0] = o_s[:256, :]
        oq3_ref[1] = dq_s[:256, :]
        for n, src in ((0, dk_s), (1, dv_s)):
            loc3_ref[n] = src[:256, :]
            to2_ref[n, 512:768, :] = src[256:512, :].astype(BF)
            to4_ref[n] = src[512:768, :].astype(BF)
            to6_ref[n] = src[768:, :].astype(BF)

    shapes = [
        ((2, 512, BLK), BF), ((2, 512, BLK), F32), ((2, 256, BLK), BF), ((2, 256, BLK), F32),
        ((2, 768, BLK), BF), ((2, 256, BLK), BF), ((2, 256, BLK), BF),
    ]
    return pl.pallas_call(
        with_order(body, 7, len(deps)),
        in_specs=[WHOLE] * 7 + [ANY] * len(deps),
        out_shape=[jax.ShapeDtypeStruct(s, d) for s, d in shapes],
        scratch_shapes=attention_scratch(512),
        compiler_params=params(),
        cost_estimate=cost(1.5 * HEAD_FLOPS, 2e6),
        name="attention_wide",
    )(keep, recv, from_2, from_4, from_6, keep_1, recv_1, *deps)


def combine_wide(oq2, loc2, oq3, loc3, ret2, ret4, ret6, out_one, deps=()):
    def body(oq2_ref, loc2_ref, oq3_ref, loc3_ref, r2_ref, r4_ref, r6_ref, one_ref, *refs):
        own_ref, back_ref, out_own, out_back = refs
        for n, (dst, out, at2, at3) in enumerate(
            ((own_ref, out_own, 0, 0), (back_ref, out_back, 256, 128))
        ):
            two = slice(at2, at2 + 256)
            three = slice(at3, at3 + 128)
            out[0:512, :] = one_ref[n]
            out[512:768, :] = oq2_ref[0, two, :]
            out[768:896, :] = oq3_ref[0, three, :]
            dst[0, 0:256, :] = oq2_ref[1, two, :]
            dst[0, 256:384, :] = oq3_ref[1, three, :]
            for n in range(2):
                dst[1 + n, 0:256, :] = (loc2_ref[n, two, :] + r2_ref[n, two, :].astype(F32)).astype(BF)
                far = r4_ref[n, three, :].astype(F32) + r6_ref[n, three, :].astype(F32)
                near = r2_ref[n, 512 + at3 : 640 + at3, :].astype(F32)
                dst[1 + n, 256:384, :] = (loc3_ref[n, three, :] + near + far).astype(BF)

    shapes = [(3, 384, BLK)] * 2 + [(896, BLK)] * 2
    return pl.pallas_call(
        with_order(body, 8, len(deps)),
        in_specs=[WHOLE] * 8 + [ANY] * len(deps),
        out_shape=[jax.ShapeDtypeStruct(shape, BF) for shape in shapes],
        compiler_params=params(),
        cost_estimate=cost(1e6, 1e4),
        name="combine_wide",
    )(oq2, loc2, oq3, loc3, ret2, ret4, ret6, out_one, *deps)


def choose_pairs(scal, sources, weight, deps=()):
    slabs = [src[0].shape[1] for src in sources]
    total = sum(slabs)

    def body(scal_ref, *refs):
        mine_ref, other_ref = refs[-2:]
        core = scal_ref[33]
        base = 0
        for n, slab in enumerate(slabs):
            first, second = refs[2 * n : 2 * n + 2]
            same = core == (0 if slab == ROWS else scal_ref[32])
            here = slice(base, base + slab)

            def copy(one, two, here=here, slot=1 if slab == ROWS else 0):
                for part in range(3):
                    mine_ref[part, here, :] = one[slot + part]
                    other_ref[part, here, :] = two[slot + part]

            pl.when(same)(lambda first=first, second=second, copy=copy: copy(first, second))
            pl.when(jnp.logical_not(same))(
                lambda first=first, second=second, copy=copy: copy(second, first)
            )
            base += slab

    flat = [x for source in sources for x in source]
    out = jax.ShapeDtypeStruct((3, total, BLK), BF)
    return pl.pallas_call(
        with_order(body, 1 + len(flat), len(deps)),
        in_specs=[pl.BlockSpec(memory_space=pltpu.SMEM)] + [WHOLE] * len(flat) + [ANY] * len(deps),
        out_shape=[out, out],
        compiler_params=params(),
        cost_estimate=cost(weight, 1e4),
        name="choose_pairs",
    )(scal, *flat, *deps)


def block_mask(block, span, off_a, off_b, low):
    here = block % span
    keep_a = jnp.where(off_a == here, 1, 0)
    keep_b = jnp.where(off_b == here, 1, 0)
    return jnp.where(low, keep_a, keep_b) == 1


def weight_grad(tokens, tokens_other, scal, groups, mine, other, weight, deps=()):
    count = len(groups) * 192
    tables = (34, 38)

    def body(scal_ref, tok_ref, tok2_ref, mine_ref, other_ref, *refs):
        outs = refs[:4]
        l_s, x_s = refs[4:]
        core = scal_ref[33]
        base = 0
        for at, group in enumerate(groups):
            span = SPANS[group]
            rows = ROWS // span
            for n, src in ((0, mine_ref), (1, other_ref)):
                to = slice(n * rows, n * rows + rows)
                for part in range(3):
                    val = src[part, base : base + rows, :].T
                    l_s[part * 64 : part * 64 + 64, to] = val[:64]
                    l_s[192 + part * 64 : 256 + part * 64, to] = val[64:]
            base += rows
            for head in range(2):
                left = l_s.at[head * 192 : head * 192 + 192, :]
                starts = [pl.multiple_of(scal_ref[tables[head] + j] * 256, 256) for j in range(4)]
                if span > 1:
                    for n, tok in ((0, tok_ref), (1, tok2_ref)):
                        off = scal_ref[n * 16 + group * 4 + 2 * core + head]
                        for r in range(8 // span):
                            row = pl.multiple_of((r * span + off) * BLK, BLK)
                            to = n * rows + r * BLK
                            for j in range(4):
                                x_s[to : to + BLK, j * 256 : j * 256 + 256] = tok[
                                    pl.ds(row, BLK), pl.ds(starts[j], 256)
                                ]
                for j in range(4):
                    if span > 1:
                        res = dot(left[:, : 2 * rows], x_s[: 2 * rows, j * 256 : j * 256 + 256])
                    else:
                        lanes = pl.ds(starts[j], 256)
                        res = dot(left[:, :ROWS], tok_ref[:, lanes])
                        res += dot(left[:, ROWS:], tok2_ref[:, lanes])
                    to = slice(at * 192, at * 192 + 192)
                    if j < 2:
                        outs[2 * head][j, to, :] = res.astype(BF)
                    else:
                        outs[2 * head + 1][j - 2, to, :] = res

    smem = pl.BlockSpec(memory_space=pltpu.SMEM)
    return pl.pallas_call(
        with_order(body, 5, len(deps)),
        in_specs=[smem] + [WHOLE] * 4 + [ANY] * len(deps),
        out_shape=[jax.ShapeDtypeStruct((2, count, 256), d) for d in (BF, F32, BF, F32)],
        scratch_shapes=[
            pltpu.VMEM((384, 2 * ROWS), BF),
            pltpu.VMEM((ROWS, 1024), BF),
        ],
        compiler_params=params(),
        cost_estimate=cost(weight, 1e4),
        name="weight_grad",
    )(scal, tokens, tokens_other, mine, other, *deps)


def fold_x(scal, keep_p, recv_p, keep_q, recv_q, deps=()):
    rows = keep_p.shape[1]

    def body(scal_ref, kp, rp, kq, rq, stay_p, leave_p, stay_q, leave_q):
        for bit, keep, recv, stay, leave in (
            (scal_ref[43], kp, rp, stay_p, leave_p),
            (scal_ref[42], kq, rq, stay_q, leave_q),
        ):
            stay[...] = keep[bit] + recv[bit].astype(F32)
            leave[...] = (keep[1 - bit] + recv[1 - bit].astype(F32)).astype(BF)

    return pl.pallas_call(
        with_order(body, 5, len(deps)),
        in_specs=[pl.BlockSpec(memory_space=pltpu.SMEM)] + [WHOLE] * 4 + [ANY] * len(deps),
        out_shape=[jax.ShapeDtypeStruct((rows, 256), d) for d in (F32, BF, F32, BF)],
        compiler_params=params(),
        cost_estimate=cost(1e6, 1e4),
        name="fold_x",
    )(scal, keep_p, recv_p, keep_q, recv_q, *deps)


def fold_y(scal, stay_p, recv_p, stay_q, recv_q, deps=()):
    rows = stay_p.shape[0]

    def body(scal_ref, sp, rp, sq, rq, stay, leave):
        bit = scal_ref[32]
        here = pl.ds(pl.multiple_of(bit * BLK, BLK), BLK)
        there = pl.ds(pl.multiple_of((1 - bit) * BLK, BLK), BLK)
        for at, own, recv in ((0, sp, rp), (rows, sq, rq)):
            stay[at : at + rows, :] = own[:, here] + recv[:, here].astype(F32)
            leave[at : at + rows, :] = (own[:, there] + recv[:, there].astype(F32)).astype(BF)

    return pl.pallas_call(
        with_order(body, 5, len(deps)),
        in_specs=[pl.BlockSpec(memory_space=pltpu.SMEM)] + [WHOLE] * 4 + [ANY] * len(deps),
        out_shape=[jax.ShapeDtypeStruct((2 * rows, BLK), d) for d in (F32, BF)],
        compiler_params=params(),
        cost_estimate=cost(1e6, 1e4),
        name="fold_y",
    )(scal, stay_p, recv_p, stay_q, recv_q, *deps)


def over_columns(left, right):
    return lax.dot_general(left, right, (((1,), (1,)), ((), ())), preferred_element_type=F32)


def token_grad(w_qkv, scal, dense, one, wide, width, piece, before=None, outs_of=(), deps=()):
    start = before is None
    last = len(outs_of) > 0

    def body(scal_ref, w_ref, d0_ref, d1_ref, o1_ref, r1_ref, ow_ref, rw_ref, *refs):
        if last:
            out_own, out_ret, dx_ref, att_ref, flag_ref, acc = refs
        else:
            dx_ref, flag_ref, acc = refs
        flag_ref[...] = jnp.zeros_like(flag_ref)
        mine = scal_ref[32]
        total = None
        for part in range(3):
            left = jnp.concatenate([d0_ref[1 + part], d1_ref[1 + part]], axis=1)
            term = over_columns(left, w_ref[:, part * 1024 : part * 1024 + 256])
            total = term if total is None else total + term
        acc[...] = total
        for group, base, own, ret in (
            (1, 0, o1_ref, r1_ref), (2, 0, ow_ref, rw_ref), (3, 256, ow_ref, rw_ref),
        ):
            span = SPANS[group]
            rows = ROWS // span
            low = first_head((rows, BLK))
            zero = jnp.zeros((), BF)
            for src, pair in ((own, mine), (ret, 1 - mine)):
                weights = []
                for part in range(3):
                    col = pl.multiple_of(part * 1024 + group * 256 + pair * BLK, BLK)
                    weights.append(w_ref[:, pl.ds(col, BLK)])
                d_q, d_k, d_v = [src[part, base : base + rows, :] for part in range(3)]
                for head in range(2):
                    if head == 0:
                        d_v_head = jnp.where(low, d_v, zero)
                    else:
                        d_v_head = jnp.where(low, zero, d_v)
                    left = head_columns(d_q, d_k, d_v_head, head)
                    res = over_columns(left, head_columns(*weights, head))
                    off = scal_ref[group * 4 + 2 * pair + head]
                    for r in range(8 // span):
                        at = pl.ds(pl.multiple_of((r * span + off) * BLK, BLK), BLK)
                        acc[at, :] += res[r * BLK : r * BLK + BLK, :]
        dx_ref[...] = acc[...].astype(BF)
        if last:
            low = first_head((BLK, BLK))
            att_ref[:, 0:BLK] = d0_ref[0]
            att_ref[:, BLK : 2 * BLK] = d1_ref[0]
            for group, base in ((1, 0), (2, 512), (3, 768)):
                span = SPANS[group]
                for src, pair in ((out_own, mine), (out_ret, 1 - mine)):
                    off_a = scal_ref[group * 4 + 2 * pair]
                    off_b = scal_ref[group * 4 + 2 * pair + 1]
                    lanes = pl.ds(pl.multiple_of(group * 256 + pair * BLK, BLK), BLK)
                    for block in range(8):
                        mask = block_mask(block, span, off_a, off_b, low)
                        row = base + (block // span) * BLK
                        val = src[row : row + BLK, :]
                        rows = slice(block * BLK, block * BLK + BLK)
                        att_ref[rows, lanes] = jnp.where(mask, val, jnp.zeros((), BF))

    out = jax.ShapeDtypeStruct((ROWS, 1024), BF)
    dx_spec = pl.BlockSpec((ROWS, width), lambda i, s: (0, piece))
    given = () if start else (before,)
    flag_spec = pl.BlockSpec((8, BLK), lambda i, s: (0, 0))
    att_spec = pl.BlockSpec((ROWS, 1024), lambda i, s: (0, 0))
    n_in = 8 + len(outs_of)
    return pl.pallas_call(
        with_order(body, n_in, len(given) + len(deps)),
        grid_spec=pltpu.PrefetchScalarGridSpec(
            num_scalar_prefetch=1,
            grid=(1,),
            in_specs=[pl.BlockSpec((width, 3072), lambda i, s: (piece, 0))]
            + [WHOLE] * (6 + len(outs_of))
            + [ANY] * (len(given) + len(deps)),
            out_specs=[dx_spec] + [att_spec] * last + [flag_spec],
            scratch_shapes=[pltpu.VMEM((ROWS, width), F32)],
        ),
        out_shape=[out] + [out] * last + [jax.ShapeDtypeStruct((8, BLK), F32)],
        input_output_aliases={} if start else {n_in: 0},
        compiler_params=params(),
        cost_estimate=cost(1e6, 1e4),
        name="token_grad",
    )(scal, w_qkv, dense[0], dense[1], one[0], one[1], wide[0], wide[1], *outs_of, *given, *deps)


def fold_add(own, recv, dtype, deps=()):
    def body(own_ref, recv_ref, out_ref):
        out_ref[...] = (own_ref[...].astype(F32) + recv_ref[...].astype(F32)).astype(dtype)

    return pl.pallas_call(
        with_order(body, 2, len(deps)),
        in_specs=[WHOLE] * 2 + [ANY] * len(deps),
        out_shape=jax.ShapeDtypeStruct(own.shape, dtype),
        compiler_params=params(),
        cost_estimate=cost(1e6, 1e4),
        name="fold_add",
    )(own, recv, *deps)


def place_weights(scal, parts, groups_of):
    def body(scal_ref, *refs):
        out = refs[-1]
        core = scal_ref[33]
        at = 0
        for groups in groups_of:
            for pair in (core, 1 - core):
                for n, group in enumerate(groups):
                    for part in range(3):
                        row = n * 192 + part * 64
                        far = len(groups) * 192 + row
                        val = jnp.concatenate(
                            [refs[at][row : row + 64, :], refs[at][far : far + 64, :]], axis=0
                        )
                        col = pl.multiple_of(part * 1024 + group * 256 + pair * BLK, BLK)
                        out[:, pl.ds(col, BLK)] = val.T
                at += 1

    return pl.pallas_call(
        body,
        in_specs=[pl.BlockSpec(memory_space=pltpu.SMEM)] + [WHOLE] * len(parts),
        out_shape=jax.ShapeDtypeStruct((BLK, 3072), F32),
        compiler_params=params(),
        cost_estimate=cost(1e6, 1e4),
        name="place_weights",
    )(scal, *parts)


def per_device(tokens, w_qkv, offsets, d_attended):
    inputs = tokens[0]
    incoming = d_attended[0]
    seq = lax.axis_index("seq")
    core = lax.axis_index("dp") & 1
    b0, b1, b2 = seq & 1, (seq >> 1) & 1, (seq >> 2) & 1
    gray = b1 ^ b2

    def start_p(j, f):
        return 2 * j + (f ^ j)

    def start_q(j, f):
        return 2 * f + j

    tail = [b0, core]
    tail += [start_p(0, 1 - gray), start_p(1, 1 - gray), start_p(0, gray), start_p(1, gray)]
    tail += [start_q(0, 1 - b2), start_q(1, 1 - b2), start_q(0, b2), start_q(1, b2)]
    tail += [b1, b2]
    tail = [jnp.asarray(t, jnp.int32) for t in tail]
    row = offsets[0]
    row_other = swap(row, "dp", 1)
    scal = jnp.concatenate([row, row, jnp.stack(tail)])
    scal_two = jnp.concatenate([row, row_other, jnp.stack(tail)])
    table_p, table_q = 34, 38

    inputs_other = swap(inputs, "dp", 1)

    keep_w, send_w = project_groups(inputs, w_qkv, scal, (2, 3))
    recv_w = swap(send_w, "seq", 1)
    keep_1, send_1, do_0 = project_groups(inputs, w_qkv, scal, (1,), (incoming,), (keep_w,))
    recv_1 = swap(send_1, "seq", 1)
    qkv_0 = project_dense(inputs, w_qkv, (keep_1, inputs_other, scal_two))

    kv_2, kv_3 = pack_pairs(keep_w, recv_w, (qkv_0,))
    from_2 = swap(kv_2, "seq", 2)
    from_4 = swap(kv_3, "seq", 4)
    from_6 = swap(kv_3, "seq", 6)

    dense_0 = attention_dense(qkv_0, do_0, 0, (kv_3,))
    wide = attention_wide(
        keep_w, recv_w, from_2, from_4, from_6, keep_1, recv_1, (dense_0,)
    )
    oq2, loc2, oq3, loc3, to2, to4, to6 = wide
    ret2 = swap(to2, "seq", 2)
    ret4 = swap(to4, "seq", 4)
    ret6 = swap(to6, "seq", 6)
    own_1, back_1, out_one = attention_two(keep_1, recv_1, (oq2,))
    ret_1 = swap(back_1, "seq", 1)
    own_w, back_w, out_own, out_back = combine_wide(
        oq2, loc2, oq3, loc3, ret2, ret4, ret6, out_one, (own_1,)
    )
    ret_w = swap(back_w, "seq", 1)
    dense_1 = attention_dense(qkv_0, do_0, 1, (own_w,))
    dense = (dense_0, dense_1)
    one = (own_1, ret_1)
    far = (own_w, ret_w)

    mine_m, other_m = choose_pairs(scal, (dense, one), 1e6)
    core_m = swap(other_m, "dp", 1)
    mine_f, other_f = choose_pairs(scal, (far,), 10e9, (mine_m,))
    core_f = swap(other_f, "dp", 1)
    grads_m = weight_grad(inputs, inputs_other, scal_two, (0, 1), mine_m, core_m, 10e9, (mine_f,))
    grads_f = weight_grad(inputs, inputs_other, scal_two, (2, 3), mine_f, core_f, 1e6, (grads_m[0],))

    def first_swap(grads):
        send_p, keep_p, send_q, keep_q = grads
        return keep_p, swap(send_p, "seq", 2), keep_q, swap(send_q, "seq", 6)

    def second_swap(folded):
        stay_p, leave_p, stay_q, leave_q = folded
        return stay_p, swap(leave_p, "seq", 6), stay_q, swap(leave_q, "seq", 2)

    def reduce_rest(total, masks):
        half = total
        for mask in masks[:2]:
            total = half.astype(F32) + swap(half, "dp", mask).astype(F32)
            half = total.astype(BF)
        total = total + swap(total, "dp", masks[2])
        return [total, swap(total, "dp", 1)]

    def tokens_part(width, piece, before, dep, outs_of=()):
        return token_grad(w_qkv, scal, dense, one, far, width, piece, before, outs_of, (dep,))

    d_part, flag = tokens_part(512, 0, None, grads_f[0])
    folded_m = fold_x(scal, *first_swap(grads_m), (flag,))
    d_part, flag = tokens_part(256, 2, d_part, folded_m[0])
    folded_f = fold_x(scal, *first_swap(grads_f), (flag,))
    stay_m, leave_m = fold_y(scal, *second_swap(folded_m), (folded_f[0],))
    stay_f, leave_f = fold_y(scal, *second_swap(folded_f), (stay_m,))
    recv_m = swap(leave_m, "seq", 1)
    recv_f = swap(leave_f, "seq", 1)
    out_ret = swap(out_back, "seq", 1)
    d_inputs, attended, flag = tokens_part(256, 3, d_part, stay_f, (out_own, out_ret))
    half_m = fold_add(stay_m, recv_m, BF, (flag,))
    half_f = fold_add(stay_f, recv_f, BF, (half_m,))
    parts = reduce_rest(half_m, (2, 6, 8)) + reduce_rest(half_f, (8, 2, 6))
    d_weights = place_weights(scal, parts, ((0, 1), (2, 3)))
    return (attended[None], d_inputs[None], d_weights)


def solution(mesh):
    placed = (P("dp", "seq", None), P(), P("dp", None), P("dp", "seq", None))
    return jax.shard_map(
        per_device,
        mesh=mesh,
        in_specs=placed,
        out_specs=(P("dp", "seq", None), P("dp", "seq", None), P("seq", None)),
        check_vma=False,
    )
```
